512 devices in a mesh: cuts: 8 (over x, core), rows: 64 (over z, y).
Axes of the slice: x: 4, y: 8, z: 8, core: 2. Of those that a mesh axis runs over, the one named last changes fastest.
Arguments:
- start_modes: float32 [8, 256, 512, 128], P('cuts', 'rows'), may hold values from -6 to 6
- contrast: float32 [8, 256, 512], P('cuts', 'rows'), may hold values from 0 to 1
- rotations: float32 [8, 2, 128, 128], P('cuts'), may hold values from -0.2 to 1.2, as said below
- ordering: int32 [8, 2, 128], P('cuts'), may hold values from 0 to 127, each once within a row
Outputs:
- modes: float32 [8, 256, 512, 128], P('cuts', 'rows')
- coupling: float32 [8, 128, 128], P('cuts', 'rows')
- rayleigh: float32 [8, 128, 128], P('cuts', 'rows')
The draws below stay inside these ranges and needn't reach their ends.
Inputs may be any that keep to these rules, and one draw needn't show every extreme that they name: `rotations`: each matrix is invertible.
All inputs are finite; a program needn't handle non-finite values.
Results may differ from the reference program's by a relative error of at most 0.00026.
Values sent between devices are 32-bit elements; how exact they have to be, the bound alone decides.
A program may use at most 64 MiB of HBM per device.

```python
import math
import jax
import jax.numpy as jnp
from jax import lax

MODES = 128
DEGREE = 4
ITERS = 2
GC = 512
SLICES = 8
GR = 256


def draw_rotations(key, part):
    spread = 0.3 / math.sqrt(MODES)
    shape = (SLICES, ITERS, MODES, MODES)
    noise = jax.random.truncated_normal(key, -4.0, 4.0, shape, jnp.float32) * spread
    identity = (jnp.arange(MODES)[:, None] == jnp.arange(MODES)[None, :]).astype(jnp.float32)
    return identity + noise


def block_levels(own_key, extent, split, smallest, high):
    level, own = 1.0, jax.random.fold_in(own_key, 6)
    for position, shards_of in split:
        heights = jnp.exp(jax.random.uniform(jax.random.fold_in(own, position), (shards_of,), jnp.float32, smallest / len(split), high / len(split)))
        level = level * jnp.repeat(heights, extent[position] // shards_of).reshape([-1 if axis == position else 1 for axis in range(len(extent))])
    return level


def bell_draw(stream_key, dims, scale, limit, split=(), kind=jnp.bfloat16):
    entries = scale * jax.random.normal(stream_key, dims, jnp.float32)
    if split:
        entries = entries * block_levels(stream_key, dims, split, -0.22, 0.18)
    return jnp.clip(entries, -limit, limit).astype(kind)


def setup_inputs(seed: int = 0) -> dict:
    key_list = jax.random.split(jax.random.key(seed), 5)
    return {
        "start_modes": bell_draw(key_list[0], (SLICES, GR, GC, MODES), 1.0, 6.0, ((0, 8), (1, 64)), jnp.float32),
        "contrast": jnp.clip(1.0 * jax.random.uniform(key_list[1], (SLICES, GR, GC), jnp.float32) ** block_levels(key_list[1], (SLICES, GR, GC), ((0, 8), (1, 64)), -0.2, 0.2), 0.0, 1.0),
        "rotations": draw_rotations(jax.random.fold_in(key_list[4], 71), 0),
        "ordering": jax.vmap(lambda own: jax.random.permutation(own, MODES))(jax.random.split(key_list[3], SLICES * ITERS)).reshape((SLICES, ITERS, MODES)).astype(jnp.int32),
    }


def neighbour_sum(center, rows_source):
    columns = jnp.pad(center, ((0, 0), (1, 1), (0, 0)))
    return rows_source[2:] + rows_source[:-2] + columns[:, 2:] + columns[:, :-2]

def operator_core(center, rows_source, section):
    return 0.8 * (section[:, :, None] * center + 0.25 * neighbour_sum(center, rows_source)) - 0.2 * center

def inner_modes(left, right):
    return jnp.einsum('rcm,rcn->mn', left, right, precision=lax.Precision.HIGHEST)

def reference(start_modes, contrast, rotations, ordering):
    pixels = GR * GC
    all_modes = []
    all_coupling = []
    all_rayleigh = []
    earlier = start_modes[0]
    for slice_id in range(SLICES):
        section = contrast[slice_id]
        subspace = start_modes[slice_id]

        def apply_full(vectors):
            return operator_core(vectors, jnp.pad(vectors, ((1, 1), (0, 0), (0, 0))), section)
        for sweep in range(ITERS):
            before = subspace
            current = apply_full(before)
            for degree_step in range(2, DEGREE + 1):
                following = 2.0 * apply_full(current) - before
                before, current = (current, following)
            filtered = current
            gram_sum = inner_modes(filtered, filtered) / pixels
            factor_low = jnp.linalg.cholesky(gram_sum)
            mixing = lax.linalg.triangular_solve(factor_low, rotations[slice_id, sweep], left_side=True, lower=True, transpose_a=True)
            picker = (ordering[slice_id, sweep][None, :] == jnp.arange(MODES, dtype=jnp.int32)[:, None]).astype(jnp.float32)
            mixing = jnp.dot(mixing, picker, precision=lax.Precision.HIGHEST)
            subspace = jnp.einsum('rcm,mn->rcn', filtered, mixing, precision=lax.Precision.HIGHEST)
        applied = apply_full(subspace)
        all_coupling.append(inner_modes(earlier, subspace) / pixels)
        all_rayleigh.append(inner_modes(subspace, applied) / pixels)
        all_modes.append(subspace)
        earlier = subspace
    return (jnp.stack(all_modes), jnp.stack(all_coupling), jnp.stack(all_rayleigh))
```

```python
import functools
import math

import jax
import jax.numpy as jnp
from jax import lax
from jax.experimental import pallas as pl
from jax.experimental.pallas import tpu as pltpu
from jax.sharding import PartitionSpec as P

DEGREE = 4
ITERS = 2
PAD = 8
MESH = pl.DeviceIdType.MESH
HIGH = lax.Precision.HIGHEST


def tdot(a, b):
    return lax.dot_general(
        a, b, (((0,), (0,)), ((), ())), precision=HIGH, preferred_element_type=jnp.float32
    )


def filter_kernel(
    v_hbm, con_hbm, f1_hbm, mats,
    e0, ya, yb, yc, e1, za, zb, zc, f1, coef, con, ctile, earlier, edge, part, land1, land2, tot,
    con_send, con_recv, h1_send, h1_recv, h2_send, h2_recv, e_send, e_recv, x_send, x_recv,
    r_send, r_recv, local,
    *, tiles, peers, slices, cuts1,
):
    rows, cols, nm = v_hbm.shape
    me = lax.axis_index("rows")
    cut = lax.axis_index("cuts")
    up = lax.rem(me + tiles - 1, tiles)
    down = lax.rem(me + 1, tiles)
    my = lax.rem(me, peers)
    mz = me // peers
    nxt = lax.rem(cut + 1, slices)
    prv = lax.rem(cut + slices - 1, slices)
    count = len(cuts1) - 1
    share = nm // peers

    def y_peer(d):
        return mz * peers + lax.rem(my + d, peers)

    def z_peer(d):
        return lax.rem(mz + d, peers) * peers + my

    barrier = pltpu.get_barrier_semaphore()
    for row in [up, down] + [y_peer(d) for d in range(1, peers)] + [z_peer(d) for d in range(1, peers)]:
        pl.semaphore_signal(barrier, inc=1, device_id={"rows": row}, device_id_type=MESH)
    for c in (nxt, prv):
        pl.semaphore_signal(barrier, inc=1, device_id={"cuts": c}, device_id_type=MESH)
    own_v = pltpu.make_async_copy(
        v_hbm, e0.at[pl.ds(rows, rows), pl.ds(PAD, cols), :], local.at[0]
    )
    own_v.start()
    own_c = pltpu.make_async_copy(con_hbm, con.at[1], local.at[1])
    own_c.start()
    pl.semaphore_wait(barrier, 2 * peers + 2)

    con_copies = []
    for side, (peer, slot) in enumerate(((up, 2), (down, 0))):
        cp = pltpu.make_async_remote_copy(
            src_ref=con_hbm, dst_ref=con.at[slot], send_sem=con_send.at[side],
            recv_sem=con_recv.at[side], device_id={"rows": peer}, device_id_type=MESH,
        )
        cp.start()
        con_copies.append(cp)

    def halo(src, dst, send, recv, index, a, b, from_hbm):
        copies = []
        for side, (peer, slot) in enumerate(((up, 2 * rows), (down, 0))):
            source = (
                src.at[:, pl.ds(a, b - a), :] if from_hbm
                else src.at[pl.ds(rows, rows), pl.ds(PAD + a, b - a), :]
            )
            cp = pltpu.make_async_remote_copy(
                src_ref=source, dst_ref=dst.at[pl.ds(slot, rows), pl.ds(PAD + a, b - a), :],
                send_sem=send.at[side, index], recv_sem=recv.at[side, index],
                device_id={"rows": peer}, device_id_type=MESH,
            )
            cp.start()
            copies.append(cp)
        return copies

    first = [
        halo(v_hbm, e0, h1_send, h1_recv, c, cuts1[c], cuts1[c + 1], True) for c in range(count)
    ]

    for ref in (e0, ya, yb, yc, e1, za, zb, zc):
        zero = jnp.zeros((ref.shape[0], PAD, nm), jnp.float32)
        ref[:, pl.ds(0, PAD), :] = zero
        ref[:, pl.ds(PAD + cols, PAD), :] = zero
    f1[:, pl.ds(cols, PAD), :] = jnp.zeros((rows, PAD, nm), jnp.float32)

    own_c.wait()
    for cp in con_copies:
        cp.wait()
    has_up = jnp.where(me > 0, 1.0, 0.0).astype(jnp.float32)
    has_down = jnp.where(me < tiles - 1, 1.0, 0.0).astype(jnp.float32)
    ctile[...] = jnp.zeros_like(ctile)
    for slot, scale in enumerate((has_up, jnp.float32(1.0), has_down)):
        ctile[pl.ds(rows * slot, rows), :] = (1.6 * con[slot] - 0.4) * scale
    for q in range(0, cols, nm):
        flipped = ctile[:, pl.ds(q, nm)].T
        for row in range(3 * rows):
            coef[row, pl.ds(q, nm), :] = jnp.broadcast_to(flipped[:, row : row + 1], (nm, nm))

    def near(i, lo):
        return jnp.where(i < -lo, 0.4 * has_up, jnp.where(i >= rows - lo, 0.4 * has_down, 0.4))

    def stage(dst, dst_off, src, src_off, prev, prev_off, dpad, lo, hi, a, b):
        if b <= a:
            return

        def one(i, _):
            at = pl.ds(PAD + a, b - a)
            s = i + (lo + src_off)
            center = src[s, at, :]
            around = (
                src[s - 1, at, :] + src[s + 1, at, :]
                + src[s, pl.ds(PAD + a - 1, b - a), :] + src[s, pl.ds(PAD + a + 1, b - a), :]
            )
            value = coef[i + (lo + rows), pl.ds(a, b - a), :] * center + near(i, lo) * around
            if prev is None:
                value = 0.5 * value
            else:
                value = value - prev[i + (lo + prev_off), at, :]
            dst[i + (lo + dst_off), pl.ds(dpad + a, b - a), :] = value
            return 0

        lax.fori_loop(0, hi - lo, one, 0)

    def sweep_block(arrays, last, last_off, last_pad, bounds):
        e, y1, y2, y3 = arrays
        (a1, b1), (a2, b2), (a3, b3), (a4, b4) = bounds
        stage(y1, 3, e, rows, None, 0, PAD, -3, rows + 3, a1, b1)
        stage(y2, 2, y1, 3, e, rows, PAD, -2, rows + 2, a2, b2)
        stage(y3, 1, y2, 2, y1, 3, PAD, -1, rows + 1, a3, b3)
        stage(last, last_off, y3, 1, y2, 2, last_pad, 0, rows, a4, b4)

    def bounds_of(edges):
        result = []
        before = [0] * DEGREE
        for c, edge_at in enumerate(edges):
            after = [
                cols if c == len(edges) - 1 else max(0, edge_at - 8 * k) for k in range(1, DEGREE + 1)
            ]
            result.append(list(zip(before, after)))
            before = after
        return result

    def blank(ref, a, b):
        @pl.when(me == 0)
        def _():
            ref[pl.ds(0, rows), pl.ds(PAD + a, b - a), :] = jnp.zeros((rows, b - a, nm), jnp.float32)

        @pl.when(me == tiles - 1)
        def _():
            ref[pl.ds(2 * rows, rows), pl.ds(PAD + a, b - a), :] = jnp.zeros(
                (rows, b - a, nm), jnp.float32
            )

    own_v.wait()
    bounds1 = bounds_of(cuts1[1:])
    second = []
    part[...] = jnp.zeros_like(part)
    for c in range(count):
        for cp in first[c]:
            cp.wait_recv()
        blank(e0, cuts1[c], cuts1[c + 1])
        sweep_block((e0, ya, yb, yc), e1, rows, PAD, bounds1[c])
        a, b = bounds1[c][-1]
        second.append(halo(e1, e1, h2_send, h2_recv, c, a, b, False))
        block = e1[pl.ds(rows, rows), pl.ds(PAD + a, b - a), :].reshape(rows * (b - a), nm)
        part[0] += tdot(block, block)

    bounds2 = bounds_of([b[-1][1] for b in bounds1])
    moved = []
    for c in range(count):
        for cp in second[c]:
            cp.wait_recv()
        blank(e1, *bounds1[c][-1])
        sweep_block((e1, za, zb, zc), f1, 0, 0, bounds2[c])
        a, b = bounds2[c][-1]
        if b > a:
            cp = pltpu.make_async_remote_copy(
                src_ref=f1.at[:, pl.ds(a, b - a), :], dst_ref=earlier.at[:, pl.ds(a, b - a), :],
                send_sem=x_send.at[c], recv_sem=x_recv.at[c],
                device_id={"cuts": nxt}, device_id_type=MESH,
            )
            cp.start()
            moved.append((cp, a, b))
            block = f1[:, pl.ds(a, b - a), :].reshape(rows * (b - a), nm)
            part[1] += tdot(block, block)
    out_f1 = pltpu.make_async_copy(f1.at[:, pl.ds(0, cols), :], f1_hbm, local.at[2])
    out_f1.start()

    half = cols // 2
    lower = pltpu.make_async_remote_copy(
        src_ref=f1.at[0, pl.ds(0, half), :], dst_ref=edge.at[0],
        send_sem=e_send.at[0], recv_sem=e_recv.at[0], device_id={"rows": up}, device_id_type=MESH,
    )
    upper = pltpu.make_async_remote_copy(
        src_ref=f1.at[rows - 1, pl.ds(half, half), :], dst_ref=edge.at[1],
        send_sem=e_send.at[1], recv_sem=e_recv.at[1], device_id={"rows": down}, device_id_type=MESH,
    )
    lower.start()
    upper.start()

    for cp, a, b in moved:
        cp.wait_recv()

        @pl.when(cut == 0)
        def _():
            earlier[:, pl.ds(a, b - a), :] = e0[pl.ds(rows, rows), pl.ds(PAD + a, b - a), :]

        part[3] += tdot(
            earlier[:, pl.ds(a, b - a), :].reshape(rows * (b - a), nm),
            f1[:, pl.ds(a, b - a), :].reshape(rows * (b - a), nm),
        )
    lower.wait_recv()
    upper.wait_recv()
    for row in range(rows):
        for q in range(0, cols, half):
            at = pl.ds(q, half)
            center = f1[row, at, :]
            g = 0.25 * coef[row + rows, at, :] * center + 0.2 * f1[row, pl.ds(q + 1, half), :]
            if row < rows - 1:
                g = g + 0.2 * f1[row + 1, at, :]
            if row == rows - 1 and q == 0:
                g = g + (0.2 * has_down) * edge[0]
            if row == 0 and q > 0:
                g = g + (0.2 * has_up) * edge[1]
            part[2] += tdot(center, g)

    waits = []
    for d in range(1, peers):
        to = lax.rem(my + d, peers)
        cp = pltpu.make_async_remote_copy(
            src_ref=part.at[:, pl.ds(to * share, share), :], dst_ref=land1.at[my],
            send_sem=r_send.at[0, d], recv_sem=r_recv.at[0, d],
            device_id={"rows": y_peer(d)}, device_id_type=MESH,
        )
        cp.start()
        waits.append(cp)
    land1[my] = part[:, pl.ds(my * share, share), :]
    for cp in waits:
        cp.wait()
    total = land1[0]
    for d in range(1, peers):
        total = total + land1[d]
    land2[mz] = total
    waits = []
    for d in range(1, peers):
        cp = pltpu.make_async_remote_copy(
            src_ref=land2.at[mz], dst_ref=land2.at[mz],
            send_sem=r_send.at[1, d], recv_sem=r_recv.at[1, d],
            device_id={"rows": z_peer(d)}, device_id_type=MESH,
        )
        cp.start()
        waits.append(cp)
    for cp in waits:
        cp.wait()
    total = land2[0]
    for d in range(1, peers):
        total = total + land2[d]
    tot[:, pl.ds(my * share, share), :] = total
    waits = []
    for d in range(1, peers):
        cp = pltpu.make_async_remote_copy(
            src_ref=tot.at[:, pl.ds(my * share, share), :],
            dst_ref=tot.at[:, pl.ds(my * share, share), :],
            send_sem=r_send.at[2, d], recv_sem=r_recv.at[2, d],
            device_id={"rows": y_peer(d)}, device_id_type=MESH,
        )
        cp.start()
        waits.append(cp)
    for cp in waits:
        cp.wait()
    mats[...] = tot[...]

    for copies in first + second:
        for cp in copies:
            cp.wait_send()
    for cp, _, _ in moved:
        cp.wait_send()
    lower.wait_send()
    upper.wait_send()
    out_f1.wait()


def run_filter(v, con):
    rows, cols, nm = v.shape
    tiles = lax.axis_size("rows")
    slices = lax.axis_size("cuts")
    peers = math.isqrt(tiles)
    width = cols // 8
    cuts1 = tuple(range(0, cols + 1, width))
    count = len(cuts1) - 1
    wide = cols + 2 * PAD
    f32 = jnp.float32
    vm = lambda *shape: pltpu.VMEM(shape, f32)
    dma = lambda *shape: pltpu.SemaphoreType.DMA(shape)
    share = nm // peers
    return pl.pallas_call(
        functools.partial(filter_kernel, tiles=tiles, peers=peers, slices=slices, cuts1=cuts1),
        out_shape=(
            jax.ShapeDtypeStruct((rows, cols, nm), f32),
            jax.ShapeDtypeStruct((4, nm, nm), f32),
        ),
        in_specs=[pl.BlockSpec(memory_space=pl.ANY)] * 2,
        out_specs=(pl.BlockSpec(memory_space=pl.ANY), pl.BlockSpec(memory_space=pltpu.VMEM)),
        scratch_shapes=[
            vm(12, wide, nm), vm(10, wide, nm), vm(8, wide, nm), vm(6, wide, nm),
            vm(12, wide, nm), vm(10, wide, nm), vm(8, wide, nm), vm(6, wide, nm),
            vm(rows, cols + PAD, nm), vm(12, cols, nm), vm(3, rows, cols), vm(nm, cols),
            vm(rows, cols, nm), vm(2, cols // 2, nm), vm(4, nm, nm),
            vm(peers, 4, share, nm), vm(peers, 4, share, nm), vm(4, nm, nm),
            dma(2), dma(2), dma(2, count), dma(2, count), dma(2, count), dma(2, count),
            dma(2), dma(2), dma(count), dma(count), dma(3, peers), dma(3, peers), dma(3),
        ],
        compiler_params=pltpu.CompilerParams(
            collective_id=0, has_side_effects=True, vmem_limit_bytes=48 * 1024 * 1024
        ),
        cost_estimate=pl.CostEstimate(flops=10**9, bytes_accessed=4 * 2**20, transcendentals=0),
        name="filtered_products",
    )(v, con)


def mix(gram, turning, order):
    nm = gram.shape[0]
    low = jnp.linalg.cholesky(gram)
    mixing = lax.linalg.triangular_solve(low, turning, left_side=True, lower=True, transpose_a=True)
    picker = (order[None, :] == jnp.arange(nm, dtype=jnp.int32)[:, None]).astype(jnp.float32)
    return jnp.dot(mixing, picker, precision=HIGH)


def body(start_modes, contrast, rotations, ordering):
    rows, cols, nm = start_modes.shape[1:]
    tiles = lax.axis_size("rows")
    slices = lax.axis_size("cuts")
    pixels = rows * tiles * cols
    f1, mats = run_filter(start_modes[0], contrast[0])
    dot = functools.partial(jnp.dot, precision=HIGH)
    mats = mats / pixels
    m0 = mix(mats[0], rotations[0, 0], ordering[0, 0])
    m1 = mix(dot(m0.T, dot(mats[1], m0)), rotations[0, 1], ordering[0, 1])
    m = dot(m0, m1)
    modes = jnp.einsum("rcm,mn->rcn", f1, m, precision=HIGH)
    share = nm // tiles
    at = lax.axis_index("rows") * share
    mine = lax.dynamic_slice_in_dim(m, at, share, 1)
    earlier = lax.ppermute(mine, "cuts", [(i, (i + 1) % slices) for i in range(slices)])
    unit = (at + jnp.arange(share)[None, :] == jnp.arange(nm)[:, None]).astype(jnp.float32)
    earlier = jnp.where(lax.axis_index("cuts") == 0, unit, earlier)
    coupling = dot(dot(earlier.T, mats[3]), m)
    rayleigh = dot(dot(mine.T, mats[2] + mats[2].T), m)
    return modes[None], coupling[None], rayleigh[None]


def solution(mesh):
    placed = (
        P("cuts", "rows", None, None),
        P("cuts", "rows", None),
        P("cuts", None, None, None),
        P("cuts", None, None),
    )
    return jax.shard_map(
        body,
        mesh=mesh,
        in_specs=placed,
        out_specs=(P("cuts", "rows", None, None), P("cuts", "rows", None), P("cuts", "rows", None)),
        check_vma=False,
    )
```

```python
import functools
import math

import jax
import jax.numpy as jnp
from jax import lax
from jax.experimental import pallas as pl
from jax.experimental.pallas import tpu as pltpu
from jax.sharding import PartitionSpec as P

DEGREE = 4
ITERS = 2
PAD = 8
MESH = pl.DeviceIdType.MESH
HIGH = lax.Precision.HIGHEST


def tdot(a, b):
    return lax.dot_general(
        a, b, (((0,), (0,)), ((), ())), precision=HIGH, preferred_element_type=jnp.float32
    )


def dot(a, b):
    return jnp.dot(a, b, precision=HIGH, preferred_element_type=jnp.float32)


def ones_where(condition):
    return jnp.where(condition, 1.0, 0.0).astype(jnp.float32)


def eliminate(gram, inverse, first, last):
    nm = gram.shape[0]
    row = lax.broadcasted_iota(jnp.int32, (8, nm), 0)
    for panel in range(first, last):
        o = 8 * panel
        rest = nm - o - 8
        sh, eh = gram[pl.ds(o, 8), :], inverse[pl.ds(o, 8), :]
        ch = [jnp.broadcast_to(sh[:, o + k : o + k + 1], (8, nm)) for k in range(8)]
        if rest:
            st, et = gram[pl.ds(o + 8, rest), :], inverse[pl.ds(o + 8, rest), :]
            ct = [jnp.broadcast_to(st[:, o + k : o + k + 1], (rest, nm)) for k in range(8)]
        pivots = jnp.ones((8, nm), jnp.float32)
        for j in range(8):
            pivot = ch[j][j : j + 1, :]
            scale = 1.0 / pivot
            pivots = jnp.where(row == j, pivot, pivots)
            rs, re = sh[j : j + 1, :], eh[j : j + 1, :]
            rc = [c[j : j + 1, :] for c in ch]
            mh = jnp.where(row > j, ch[j] * scale, 0.0)
            for k in range(j + 1, 8):
                ch[k] = ch[k] - mh * rc[k]
            sh = sh - mh * rs
            eh = eh - mh * re
            if rest:
                mt = ct[j] * scale
                for k in range(j + 1, 8):
                    ct[k] = ct[k] - mt * rc[k]
                st = st - mt * rs
                et = et - mt * re
        inverse[pl.ds(o, 8), :] = eh * lax.rsqrt(pivots)
        if rest:
            gram[pl.ds(o + 8, rest), :] = st
            inverse[pl.ds(o + 8, rest), :] = et


def lantern_kernel(
    v_hbm, con_hbm, rot_hbm, order_hbm, modes_hbm, coupling_out, rayleigh_out,
    e0, ya, yb, yc, e1, za, zb, zc, f1, coef, con, ctile, earlier, edge, vout,
    part0, part1, part2, landa, landb, tot0, tot1, tot2, rot, order, gram, inverse, m0, mine, before,
    con_send, con_recv, h1_send, h1_recv, h2_send, h2_recv, e_send, e_recv, x_send, x_recv,
    r_send, r_recv, m_send, m_recv, local,
    *, tiles, peers, slices, cuts1,
):
    rows, cols, nm = v_hbm.shape
    me = lax.axis_index("rows")
    cut = lax.axis_index("cuts")
    up = lax.rem(me + tiles - 1, tiles)
    down = lax.rem(me + 1, tiles)
    my = lax.rem(me, peers)
    mz = me // peers
    nxt = lax.rem(cut + 1, slices)
    prv = lax.rem(cut + slices - 1, slices)
    count = len(cuts1) - 1
    share = nm // peers

    def y_peer(d):
        return mz * peers + lax.rem(my + d, peers)

    def z_peer(d):
        return lax.rem(mz + d, peers) * peers + my

    barrier = pltpu.get_barrier_semaphore()
    for row in [up, down] + [y_peer(d) for d in range(1, peers)] + [z_peer(d) for d in range(1, peers)]:
        pl.semaphore_signal(barrier, inc=1, device_id={"rows": row}, device_id_type=MESH)
    for c in (nxt, prv):
        pl.semaphore_signal(barrier, inc=1, device_id={"cuts": c}, device_id_type=MESH)
    own_v = pltpu.make_async_copy(
        v_hbm, e0.at[pl.ds(rows, rows), pl.ds(PAD, cols), :], local.at[0]
    )
    own_v.start()
    own_c = pltpu.make_async_copy(con_hbm, con.at[1], local.at[1])
    own_c.start()
    own_r = pltpu.make_async_copy(rot_hbm, rot, local.at[2])
    own_r.start()
    own_o = pltpu.make_async_copy(order_hbm, order, local.at[3])
    own_o.start()
    pl.semaphore_wait(barrier, 2 * peers + 2)

    con_copies = []
    for side, (peer, slot) in enumerate(((up, 2), (down, 0))):
        cp = pltpu.make_async_remote_copy(
            src_ref=con_hbm, dst_ref=con.at[slot], send_sem=con_send.at[side],
            recv_sem=con_recv.at[side], device_id={"rows": peer}, device_id_type=MESH,
        )
        cp.start()
        con_copies.append(cp)

    def halo(src, dst, send, recv, index, a, b, from_hbm):
        copies = []
        for side, (peer, slot) in enumerate(((up, 2 * rows), (down, 0))):
            source = (
                src.at[:, pl.ds(a, b - a), :] if from_hbm
                else src.at[pl.ds(rows, rows), pl.ds(PAD + a, b - a), :]
            )
            cp = pltpu.make_async_remote_copy(
                src_ref=source, dst_ref=dst.at[pl.ds(slot, rows), pl.ds(PAD + a, b - a), :],
                send_sem=send.at[side, index], recv_sem=recv.at[side, index],
                device_id={"rows": peer}, device_id_type=MESH,
            )
            cp.start()
            copies.append(cp)
        return copies

    first = [
        halo(v_hbm, e0, h1_send, h1_recv, c, cuts1[c], cuts1[c + 1], True) for c in range(count)
    ]

    for ref in (e0, ya, yb, yc, e1, za, zb, zc):
        zero = jnp.zeros((ref.shape[0], PAD, nm), jnp.float32)
        ref[:, pl.ds(0, PAD), :] = zero
        ref[:, pl.ds(PAD + cols, PAD), :] = zero
    f1[:, pl.ds(cols, PAD), :] = jnp.zeros((rows, PAD, nm), jnp.float32)

    own_c.wait()
    for cp in con_copies:
        cp.wait()
    has_up = jnp.where(me > 0, 1.0, 0.0).astype(jnp.float32)
    has_down = jnp.where(me < tiles - 1, 1.0, 0.0).astype(jnp.float32)
    ctile[...] = jnp.zeros_like(ctile)
    for slot, scale in enumerate((has_up, jnp.float32(1.0), has_down)):
        ctile[pl.ds(rows * slot, rows), :] = (1.6 * con[slot] - 0.4) * scale
    for q in range(0, cols, nm):
        flipped = ctile[:, pl.ds(q, nm)].T
        for row in range(3 * rows):
            coef[row, pl.ds(q, nm), :] = jnp.broadcast_to(flipped[:, row : row + 1], (nm, nm))

    own_r.wait()
    own_o.wait()
    index = lax.broadcasted_iota(jnp.int32, (nm, nm), 0)
    for t in range(ITERS):
        picker = ones_where(index == jnp.broadcast_to(order[pl.ds(t, 1), :], (nm, nm)))
        rot[t] = dot(rot[t], picker)
    unit = ones_where(index == lax.broadcasted_iota(jnp.int32, (nm, nm), 1))

    def near(i, lo):
        return jnp.where(i < -lo, 0.4 * has_up, jnp.where(i >= rows - lo, 0.4 * has_down, 0.4))

    def stage(dst, dst_off, src, src_off, prev, prev_off, dpad, lo, hi, a, b):
        if b <= a:
            return

        def one(i, _):
            at = pl.ds(PAD + a, b - a)
            s = i + (lo + src_off)
            center = src[s, at, :]
            around = (
                src[s - 1, at, :] + src[s + 1, at, :]
                + src[s, pl.ds(PAD + a - 1, b - a), :] + src[s, pl.ds(PAD + a + 1, b - a), :]
            )
            value = coef[i + (lo + rows), pl.ds(a, b - a), :] * center + near(i, lo) * around
            if prev is None:
                value = 0.5 * value
            else:
                value = value - prev[i + (lo + prev_off), at, :]
            dst[i + (lo + dst_off), pl.ds(dpad + a, b - a), :] = value
            return 0

        lax.fori_loop(0, hi - lo, one, 0)

    def sweep_block(arrays, last, last_off, last_pad, bounds):
        e, y1, y2, y3 = arrays
        (a1, b1), (a2, b2), (a3, b3), (a4, b4) = bounds
        stage(y1, 3, e, rows, None, 0, PAD, -3, rows + 3, a1, b1)
        stage(y2, 2, y1, 3, e, rows, PAD, -2, rows + 2, a2, b2)
        stage(y3, 1, y2, 2, y1, 3, PAD, -1, rows + 1, a3, b3)
        stage(last, last_off, y3, 1, y2, 2, last_pad, 0, rows, a4, b4)

    def bounds_of(edges):
        result = []
        before = [0] * DEGREE
        for c, edge_at in enumerate(edges):
            after = [
                cols if c == len(edges) - 1 else max(0, edge_at - 8 * k) for k in range(1, DEGREE + 1)
            ]
            result.append(list(zip(before, after)))
            before = after
        return result

    def blank(ref, a, b):
        @pl.when(me == 0)
        def _():
            ref[pl.ds(0, rows), pl.ds(PAD + a, b - a), :] = jnp.zeros((rows, b - a, nm), jnp.float32)

        @pl.when(me == tiles - 1)
        def _():
            ref[pl.ds(2 * rows, rows), pl.ds(PAD + a, b - a), :] = jnp.zeros(
                (rows, b - a, nm), jnp.float32
            )

    def summing(which, part, total):
        count = part.shape[0]
        lo = sum((1, 1, 2)[:which])
        land1 = landa.at[:, pl.ds(lo, count)]
        land2 = landb.at[:, pl.ds(lo, count)]
        ours = pl.ds(my * share, share)
        started = []

        def send(step, d, src, dst, row):
            cp = pltpu.make_async_remote_copy(
                src_ref=src, dst_ref=dst, send_sem=r_send.at[which, step, d],
                recv_sem=r_recv.at[which, step, d], device_id={"rows": row}, device_id_type=MESH,
            )
            cp.start()
            started.append(cp)

        def finish():
            for cp in started:
                cp.wait()
            started.clear()

        def added(land):
            value = land[0]
            for d in range(1, peers):
                value = value + land[d]
            return value

        def spread():
            for d in range(1, peers):
                to = pl.ds(lax.rem(my + d, peers) * share, share)
                send(0, d, part.at[:, to, :], land1.at[my], y_peer(d))
            land1[my] = part[:, ours, :]

        def across():
            finish()
            land2[mz] = added(land1)
            for d in range(1, peers):
                send(1, d, land2.at[mz], land2.at[mz], z_peer(d))

        def gather():
            finish()
            total[:, ours, :] = added(land2) * (1.0 / (rows * tiles * cols))
            for d in range(1, peers):
                send(2, d, total.at[:, ours, :], total.at[:, ours, :], y_peer(d))

        return spread, across, gather, finish

    sum0 = summing(0, part0, tot0)
    sum1 = summing(1, part1, tot1)
    sum2 = summing(2, part2, tot2)

    own_v.wait()
    bounds1 = bounds_of(cuts1[1:])
    second = []
    for ref in (part0, part1, part2):
        ref[...] = jnp.zeros_like(ref)
    for c in range(count):
        for cp in first[c]:
            cp.wait_recv()
        blank(e0, cuts1[c], cuts1[c + 1])
        sweep_block((e0, ya, yb, yc), e1, rows, PAD, bounds1[c])
        a, b = bounds1[c][-1]
        second.append(halo(e1, e1, h2_send, h2_recv, c, a, b, False))
        block = e1[pl.ds(rows, rows), pl.ds(PAD + a, b - a), :].reshape(rows * (b - a), nm)
        part0[0] += tdot(block, block)
    sum0[0]()

    def start_inverse(value):
        gram[...] = value
        inverse[...] = unit

    def first_mixing():
        eliminate(gram, inverse, third * 2, nm // 8)
        m0[...] = tdot(inverse[...], rot[0])

    third = nm // 24
    between = {
        0: sum0[1],
        1: sum0[2],
        2: lambda: (sum0[3](), start_inverse(tot0[0]), eliminate(gram, inverse, 0, third)),
        3: lambda: eliminate(gram, inverse, third, third * 2),
        4: first_mixing,
    }

    def correlate(item):
        cp, a, b = item
        cp.wait_recv()

        @pl.when(cut == 0)
        def _():
            earlier[:, pl.ds(a, b - a), :] = e0[pl.ds(rows, rows), pl.ds(PAD + a, b - a), :]

        part2[1] += tdot(
            earlier[:, pl.ds(a, b - a), :].reshape(rows * (b - a), nm),
            f1[:, pl.ds(a, b - a), :].reshape(rows * (b - a), nm),
        )

    bounds2 = bounds_of([b[-1][1] for b in bounds1])
    moved = []
    for c in range(count):
        for cp in second[c]:
            cp.wait_recv()
        blank(e1, *bounds1[c][-1])
        sweep_block((e1, za, zb, zc), f1, 0, 0, bounds2[c])
        a, b = bounds2[c][-1]
        if b > a:
            cp = pltpu.make_async_remote_copy(
                src_ref=f1.at[:, pl.ds(a, b - a), :], dst_ref=earlier.at[:, pl.ds(a, b - a), :],
                send_sem=x_send.at[c], recv_sem=x_recv.at[c],
                device_id={"cuts": nxt}, device_id_type=MESH,
            )
            cp.start()
            moved.append((cp, a, b))
            block = f1[:, pl.ds(a, b - a), :].reshape(rows * (b - a), nm)
            part1[0] += tdot(block, block)
        if len(moved) > 2:
            correlate(moved[len(moved) - 3])
        if c in between:
            between[c]()
    sum1[0]()

    half = cols // 2
    lower = pltpu.make_async_remote_copy(
        src_ref=f1.at[0, pl.ds(0, half), :], dst_ref=edge.at[0],
        send_sem=e_send.at[0], recv_sem=e_recv.at[0], device_id={"rows": up}, device_id_type=MESH,
    )
    upper = pltpu.make_async_remote_copy(
        src_ref=f1.at[rows - 1, pl.ds(half, half), :], dst_ref=edge.at[1],
        send_sem=e_send.at[1], recv_sem=e_recv.at[1], device_id={"rows": down}, device_id_type=MESH,
    )
    lower.start()
    upper.start()

    for item in moved[-2:]:
        correlate(item)
    sum1[1]()
    lower.wait_recv()
    upper.wait_recv()
    for row in range(rows):
        for q in range(0, cols, half):
            at = pl.ds(q, half)
            center = f1[row, at, :]
            g = 0.25 * coef[row + rows, at, :] * center + 0.2 * f1[row, pl.ds(q + 1, half), :]
            if row < rows - 1:
                g = g + 0.2 * f1[row + 1, at, :]
            if row == rows - 1 and q == 0:
                g = g + (0.2 * has_down) * edge[0]
            if row == 0 and q > 0:
                g = g + (0.2 * has_up) * edge[1]
            part2[0] += tdot(center, g)
        if row == rows // 2 - 1:
            sum1[2]()
    sum2[0]()

    sum1[3]()
    start_inverse(tdot(m0[...], dot(tot1[0], m0[...])))
    eliminate(gram, inverse, 0, third)
    sum2[1]()
    eliminate(gram, inverse, third, third * 2)
    sum2[2]()
    eliminate(gram, inverse, third * 2, nm // 8)
    mixing = dot(m0[...], tdot(inverse[...], rot[1]))
    picked = mine.shape[0]
    at = me * (nm // tiles)
    chosen = ones_where(
        lax.broadcasted_iota(jnp.int32, (picked, nm), 0) + at
        == lax.broadcasted_iota(jnp.int32, (picked, nm), 1)
    )
    mine[...] = lax.dot_general(
        chosen, mixing, (((1,), (1,)), ((), ())), precision=HIGH, preferred_element_type=jnp.float32
    )
    onward = pltpu.make_async_remote_copy(
        src_ref=mine, dst_ref=before, send_sem=m_send, recv_sem=m_recv,
        device_id={"cuts": nxt}, device_id_type=MESH,
    )
    onward.start()
    outs = []
    for row in range(rows):
        vout[row] = dot(f1[row, pl.ds(0, cols), :], mixing)
        cp = pltpu.make_async_copy(vout.at[row], modes_hbm.at[row], local.at[4 + row])
        cp.start()
        outs.append(cp)
    sum2[3]()
    both = tot2[0]
    rayleigh_out[...] = dot(dot(mine[...], both + both.T), mixing)
    onward.wait()
    left = jnp.where(cut == 0, chosen, before[...])
    coupling_out[...] = dot(dot(left, tot2[1]), mixing)

    for copies in first + second:
        for cp in copies:
            cp.wait_send()
    for cp, _, _ in moved:
        cp.wait_send()
    lower.wait_send()
    upper.wait_send()
    for cp in outs:
        cp.wait()


def body(start_modes, contrast, rotations, ordering):
    rows, cols, nm = start_modes.shape[1:]
    tiles = lax.axis_size("rows")
    slices = lax.axis_size("cuts")
    peers = math.isqrt(tiles)
    width = cols // 8
    cuts1 = tuple(range(0, cols + 1, width))
    count = len(cuts1) - 1
    wide = cols + 2 * PAD
    f32 = jnp.float32
    vm = lambda *shape: pltpu.VMEM(shape, f32)
    dma = lambda *shape: pltpu.SemaphoreType.DMA(shape)
    share = nm // peers
    kept = nm // tiles
    picked = max(8, kept)
    hbm = pl.BlockSpec(memory_space=pltpu.HBM)
    modes, coupling, rayleigh = pl.pallas_call(
        functools.partial(lantern_kernel, tiles=tiles, peers=peers, slices=slices, cuts1=cuts1),
        out_shape=(
            jax.ShapeDtypeStruct((rows, cols, nm), f32),
            jax.ShapeDtypeStruct((picked, nm), f32),
            jax.ShapeDtypeStruct((picked, nm), f32),
        ),
        in_specs=[hbm] * 4,
        out_specs=(hbm,) + (pl.BlockSpec(memory_space=pltpu.VMEM),) * 2,
        scratch_shapes=[
            vm(12, wide, nm), vm(10, wide, nm), vm(8, wide, nm), vm(6, wide, nm),
            vm(12, wide, nm), vm(10, wide, nm), vm(8, wide, nm), vm(6, wide, nm),
            vm(rows, cols + PAD, nm), vm(12, cols, nm), vm(3, rows, cols), vm(nm, cols),
            vm(rows, cols, nm), vm(2, cols // 2, nm), vm(rows, cols, nm),
            vm(1, nm, nm), vm(1, nm, nm), vm(2, nm, nm),
            vm(peers, 4, share, nm), vm(peers, 4, share, nm),
            vm(1, nm, nm), vm(1, nm, nm), vm(2, nm, nm),
            vm(ITERS, nm, nm), pltpu.VMEM((ITERS, nm), jnp.int32),
            vm(nm, nm), vm(nm, nm), vm(nm, nm), vm(picked, nm), vm(picked, nm),
            dma(2), dma(2), dma(2, count), dma(2, count), dma(2, count), dma(2, count),
            dma(2), dma(2), dma(count), dma(count), dma(3, 3, peers), dma(3, 3, peers),
            pltpu.SemaphoreType.DMA, pltpu.SemaphoreType.DMA, dma(4 + rows),
        ],
        compiler_params=pltpu.CompilerParams(
            collective_id=0, has_side_effects=True, vmem_limit_bytes=56 * 1024 * 1024
        ),
        cost_estimate=pl.CostEstimate(flops=10**9, bytes_accessed=4 * 2**20, transcendentals=0),
        name="lantern",
    )(start_modes[0], contrast[0], rotations[0], ordering[0])
    return modes[None], coupling[None, :kept], rayleigh[None, :kept]


def solution(mesh):
    placed = (
        P("cuts", "rows", None, None),
        P("cuts", "rows", None),
        P("cuts", None, None, None),
        P("cuts", None, None),
    )
    return jax.shard_map(
        body,
        mesh=mesh,
        in_specs=placed,
        out_specs=(P("cuts", "rows", None, None), P("cuts", "rows", None), P("cuts", "rows", None)),
        check_vma=False,
    )
```

```python
import functools
import math

import jax
import jax.numpy as jnp
from jax import lax
from jax.experimental import pallas as pl
from jax.experimental.pallas import tpu as pltpu
from jax.sharding import PartitionSpec as P

DEGREE = 4
ITERS = 2
PAD = 8
AHEAD = 2
MESH = pl.DeviceIdType.MESH
HIGH = lax.Precision.HIGHEST


def tdot(a, b):
    return lax.dot_general(
        a, b, (((0,), (0,)), ((), ())), precision=HIGH, preferred_element_type=jnp.float32
    )


def dot(a, b):
    return jnp.dot(a, b, precision=HIGH, preferred_element_type=jnp.float32)


def ones_where(condition):
    return jnp.where(condition, 1.0, 0.0).astype(jnp.float32)


def eliminate(gram, inverse, first, last):
    nm = gram.shape[0]
    row = lax.broadcasted_iota(jnp.int32, (8, nm), 0)
    for panel in range(first, last):
        o = 8 * panel
        rest = nm - o - 8
        sh, eh = gram[pl.ds(o, 8), :], inverse[pl.ds(o, 8), :]
        ch = [jnp.broadcast_to(sh[:, o + k : o + k + 1], (8, nm)) for k in range(8)]
        if rest:
            st, et = gram[pl.ds(o + 8, rest), :], inverse[pl.ds(o + 8, rest), :]
            ct = [jnp.broadcast_to(st[:, o + k : o + k + 1], (rest, nm)) for k in range(8)]
        pivots = jnp.ones((8, nm), jnp.float32)
        for j in range(8):
            pivot = ch[j][j : j + 1, :]
            scale = 1.0 / pivot
            pivots = jnp.where(row == j, pivot, pivots)
            rs, re = sh[j : j + 1, :], eh[j : j + 1, :]
            rc = [c[j : j + 1, :] for c in ch]
            mh = jnp.where(row > j, ch[j] * scale, 0.0)
            for k in range(j + 1, 8):
                ch[k] = ch[k] - mh * rc[k]
            sh = sh - mh * rs
            eh = eh - mh * re
            if rest:
                mt = ct[j] * scale
                for k in range(j + 1, 8):
                    ct[k] = ct[k] - mt * rc[k]
                st = st - mt * rs
                et = et - mt * re
        inverse[pl.ds(o, 8), :] = eh * lax.rsqrt(pivots)
        if rest:
            gram[pl.ds(o + 8, rest), :] = st
            inverse[pl.ds(o + 8, rest), :] = et


def lantern_kernel(
    v_hbm, con_hbm, rot_hbm, order_hbm, modes_out, coupling_out, rayleigh_out,
    e0, ya, yb, yc, e1, za, zb, zc, f1, coef, con, ctile, earlier, edge,
    part0, part1, part2, landa, landb, tot0, tot1, tot2, rot, order, gram, inverse, m0, mine, before,
    con_send, con_recv, h1_send, h1_recv, h2_send, h2_recv, e_send, e_recv, x_send, x_recv,
    r_send, r_recv, m_send, m_recv, local,
    *, tiles, peers, slices, cuts1,
):
    rows, cols, nm = v_hbm.shape
    me = lax.axis_index("rows")
    cut = lax.axis_index("cuts")
    up = lax.rem(me + tiles - 1, tiles)
    down = lax.rem(me + 1, tiles)
    my = lax.rem(me, peers)
    mz = me // peers
    nxt = lax.rem(cut + 1, slices)
    prv = lax.rem(cut + slices - 1, slices)
    count = len(cuts1) - 1
    share = nm // peers

    def y_peer(d):
        return mz * peers + lax.rem(my + d, peers)

    def z_peer(d):
        return lax.rem(mz + d, peers) * peers + my

    barrier = pltpu.get_barrier_semaphore()
    for row in [up, down] + [y_peer(d) for d in range(1, peers)] + [z_peer(d) for d in range(1, peers)]:
        pl.semaphore_signal(barrier, inc=1, device_id={"rows": row}, device_id_type=MESH)
    for c in (nxt, prv):
        pl.semaphore_signal(barrier, inc=1, device_id={"cuts": c}, device_id_type=MESH)
    own_v = pltpu.make_async_copy(
        v_hbm, e0.at[pl.ds(rows, rows), pl.ds(PAD, cols), :], local.at[0]
    )
    own_v.start()
    own_c = pltpu.make_async_copy(con_hbm, con.at[1], local.at[1])
    own_c.start()
    own_r = pltpu.make_async_copy(rot_hbm, rot, local.at[2])
    own_r.start()
    own_o = pltpu.make_async_copy(order_hbm, order, local.at[3])
    own_o.start()
    pl.semaphore_wait(barrier, 2 * peers + 2)

    con_copies = []
    for side, (peer, slot) in enumerate(((up, 2), (down, 0))):
        cp = pltpu.make_async_remote_copy(
            src_ref=con_hbm, dst_ref=con.at[slot], send_sem=con_send.at[side],
            recv_sem=con_recv.at[side], device_id={"rows": peer}, device_id_type=MESH,
        )
        cp.start()
        con_copies.append(cp)

    def halo(src, dst, send, recv, index, a, b, from_hbm):
        copies = []
        for side, (peer, slot) in enumerate(((up, 2 * rows), (down, 0))):
            source = (
                src.at[:, pl.ds(a, b - a), :] if from_hbm
                else src.at[pl.ds(rows, rows), pl.ds(PAD + a, b - a), :]
            )
            cp = pltpu.make_async_remote_copy(
                src_ref=source, dst_ref=dst.at[pl.ds(slot, rows), pl.ds(PAD + a, b - a), :],
                send_sem=send.at[side, index], recv_sem=recv.at[side, index],
                device_id={"rows": peer}, device_id_type=MESH,
            )
            cp.start()
            copies.append(cp)
        return copies

    first = [
        halo(v_hbm, e0, h1_send, h1_recv, c, cuts1[c], cuts1[c + 1], True) for c in range(count)
    ]

    for ref in (e0, ya, yb, yc, e1, za, zb, zc):
        zero = jnp.zeros((ref.shape[0], PAD, nm), jnp.float32)
        ref[:, pl.ds(0, PAD), :] = zero
        ref[:, pl.ds(PAD + cols, PAD), :] = zero
    f1[:, pl.ds(cols, PAD), :] = jnp.zeros((rows, PAD, nm), jnp.float32)

    own_c.wait()
    for cp in con_copies:
        cp.wait()
    has_up = jnp.where(me > 0, 1.0, 0.0).astype(jnp.float32)
    has_down = jnp.where(me < tiles - 1, 1.0, 0.0).astype(jnp.float32)
    ctile[...] = jnp.zeros_like(ctile)
    for slot, scale in enumerate((has_up, jnp.float32(1.0), has_down)):
        ctile[pl.ds(rows * slot, rows), :] = (1.6 * con[slot] - 0.4) * scale
    for q in range(0, cols, nm):
        flipped = ctile[:, pl.ds(q, nm)].T
        for row in range(3 * rows):
            coef[row, pl.ds(q, nm), :] = jnp.broadcast_to(flipped[:, row : row + 1], (nm, nm))

    own_r.wait()
    own_o.wait()
    index = lax.broadcasted_iota(jnp.int32, (nm, nm), 0)
    for t in range(ITERS):
        picker = ones_where(index == jnp.broadcast_to(order[pl.ds(t, 1), :], (nm, nm)))
        rot[t] = dot(rot[t], picker)
    unit = ones_where(index == lax.broadcasted_iota(jnp.int32, (nm, nm), 1))

    def near(i, lo):
        return jnp.where(i < -lo, 0.4 * has_up, jnp.where(i >= rows - lo, 0.4 * has_down, 0.4))

    def stage(dst, dst_off, src, src_off, prev, prev_off, dpad, lo, hi, a, b):
        if b <= a:
            return

        def one(i, _):
            at = pl.ds(PAD + a, b - a)
            s = i + (lo + src_off)
            center = src[s, at, :]
            around = (
                src[s - 1, at, :] + src[s + 1, at, :]
                + src[s, pl.ds(PAD + a - 1, b - a), :] + src[s, pl.ds(PAD + a + 1, b - a), :]
            )
            value = coef[i + (lo + rows), pl.ds(a, b - a), :] * center + near(i, lo) * around
            if prev is None:
                value = 0.5 * value
            else:
                value = value - prev[i + (lo + prev_off), at, :]
            dst[i + (lo + dst_off), pl.ds(dpad + a, b - a), :] = value
            return 0

        lax.fori_loop(0, hi - lo, one, 0)

    def sweep_block(arrays, last, last_off, last_pad, bounds):
        e, y1, y2, y3 = arrays
        (a1, b1), (a2, b2), (a3, b3), (a4, b4) = bounds
        stage(y1, 3, e, rows, None, 0, PAD, -3, rows + 3, a1, b1)
        stage(y2, 2, y1, 3, e, rows, PAD, -2, rows + 2, a2, b2)
        stage(y3, 1, y2, 2, y1, 3, PAD, -1, rows + 1, a3, b3)
        stage(last, last_off, y3, 1, y2, 2, last_pad, 0, rows, a4, b4)

    def bounds_of(edges):
        result = []
        before = [0] * DEGREE
        for c, edge_at in enumerate(edges):
            after = [
                cols if c == len(edges) - 1 else max(0, edge_at - 8 * k) for k in range(1, DEGREE + 1)
            ]
            result.append(list(zip(before, after)))
            before = after
        return result

    def blank(ref, a, b):
        @pl.when(me == 0)
        def _():
            ref[pl.ds(0, rows), pl.ds(PAD + a, b - a), :] = jnp.zeros((rows, b - a, nm), jnp.float32)

        @pl.when(me == tiles - 1)
        def _():
            ref[pl.ds(2 * rows, rows), pl.ds(PAD + a, b - a), :] = jnp.zeros(
                (rows, b - a, nm), jnp.float32
            )

    def summing(which, part, total):
        count = part.shape[0]
        lo = sum((1, 1, 2)[:which])
        land1 = landa.at[:, pl.ds(lo, count)]
        land2 = landb.at[:, pl.ds(lo, count)]
        ours = pl.ds(my * share, share)
        started = []

        def send(step, d, src, dst, row):
            cp = pltpu.make_async_remote_copy(
                src_ref=src, dst_ref=dst, send_sem=r_send.at[which, step, d],
                recv_sem=r_recv.at[which, step, d], device_id={"rows": row}, device_id_type=MESH,
            )
            cp.start()
            started.append(cp)

        def finish():
            for cp in started:
                cp.wait()
            started.clear()

        def added(land):
            value = land[0]
            for d in range(1, peers):
                value = value + land[d]
            return value

        def spread():
            for d in range(1, peers):
                to = pl.ds(lax.rem(my + d, peers) * share, share)
                send(0, d, part.at[:, to, :], land1.at[my], y_peer(d))
            land1[my] = part[:, ours, :]

        def across():
            finish()
            land2[mz] = added(land1)
            for d in range(1, peers):
                send(1, d, land2.at[mz], land2.at[mz], z_peer(d))

        def gather():
            finish()
            total[:, ours, :] = added(land2) * (1.0 / (rows * tiles * cols))
            for d in range(1, peers):
                send(2, d, total.at[:, ours, :], total.at[:, ours, :], y_peer(d))

        return spread, across, gather, finish

    sum0 = summing(0, part0, tot0)
    sum1 = summing(1, part1, tot1)
    sum2 = summing(2, part2, tot2)

    own_v.wait()
    bounds1 = bounds_of(cuts1[1:])
    second = []
    for ref in (part0, part1, part2):
        ref[...] = jnp.zeros_like(ref)
    for c in range(count):
        for cp in first[c]:
            cp.wait_recv()
        blank(e0, cuts1[c], cuts1[c + 1])
        sweep_block((e0, ya, yb, yc), e1, rows, PAD, bounds1[c])
        a, b = bounds1[c][-1]
        if c < AHEAD:
            second.append(halo(e1, e1, h2_send, h2_recv, c, a, b, False))
        block = e1[pl.ds(rows, rows), pl.ds(PAD + a, b - a), :].reshape(rows * (b - a), nm)
        part0[0] += tdot(block, block)
    sum0[0]()

    def start_inverse(value):
        gram[...] = value
        inverse[...] = unit

    def first_mixing():
        sum0[3]()
        start_inverse(tot0[0])
        eliminate(gram, inverse, 0, nm // 8)
        m0[...] = tdot(inverse[...], rot[0])

    third = nm // 24
    between = {3: sum0[1], 6: sum0[2]}

    def correlate(item):
        cp, a, b = item
        cp.wait_recv()

        @pl.when(cut == 0)
        def _():
            earlier[:, pl.ds(a, b - a), :] = e0[pl.ds(rows, rows), pl.ds(PAD + a, b - a), :]

        part2[1] += tdot(
            earlier[:, pl.ds(a, b - a), :].reshape(rows * (b - a), nm),
            f1[:, pl.ds(a, b - a), :].reshape(rows * (b - a), nm),
        )

    bounds2 = bounds_of([b[-1][1] for b in bounds1])
    moved = []
    for c in range(count):
        for cp in second[c]:
            cp.wait_recv()
        if c + AHEAD < count:
            second.append(halo(e1, e1, h2_send, h2_recv, c + AHEAD, *bounds1[c + AHEAD][-1], False))
        blank(e1, *bounds1[c][-1])
        sweep_block((e1, za, zb, zc), f1, 0, 0, bounds2[c])
        a, b = bounds2[c][-1]
        if b > a:
            cp = pltpu.make_async_remote_copy(
                src_ref=f1.at[:, pl.ds(a, b - a), :], dst_ref=earlier.at[:, pl.ds(a, b - a), :],
                send_sem=x_send.at[c], recv_sem=x_recv.at[c],
                device_id={"cuts": nxt}, device_id_type=MESH,
            )
            cp.start()
            moved.append((cp, a, b))
            block = f1[:, pl.ds(a, b - a), :].reshape(rows * (b - a), nm)
            part1[0] += tdot(block, block)
        if len(moved) > 2:
            correlate(moved[len(moved) - 3])
        if c in between:
            between[c]()
    sum1[0]()

    half = cols // 2
    lower = pltpu.make_async_remote_copy(
        src_ref=f1.at[0, pl.ds(0, half), :], dst_ref=edge.at[0],
        send_sem=e_send.at[0], recv_sem=e_recv.at[0], device_id={"rows": up}, device_id_type=MESH,
    )
    upper = pltpu.make_async_remote_copy(
        src_ref=f1.at[rows - 1, pl.ds(half, half), :], dst_ref=edge.at[1],
        send_sem=e_send.at[1], recv_sem=e_recv.at[1], device_id={"rows": down}, device_id_type=MESH,
    )
    lower.start()
    upper.start()

    for item in moved[-2:]:
        correlate(item)
    first_mixing()
    sum1[1]()
    lower.wait_recv()
    upper.wait_recv()
    for row in range(rows):
        for q in range(0, cols, half):
            at = pl.ds(q, half)
            center = f1[row, at, :]
            g = 0.25 * coef[row + rows, at, :] * center + 0.2 * f1[row, pl.ds(q + 1, half), :]
            if row < rows - 1:
                g = g + 0.2 * f1[row + 1, at, :]
            if row == rows - 1 and q == 0:
                g = g + (0.2 * has_down) * edge[0]
            if row == 0 and q > 0:
                g = g + (0.2 * has_up) * edge[1]
            part2[0] += tdot(center, g)
    sum1[2]()
    sum2[0]()

    sum1[3]()
    start_inverse(tdot(m0[...], dot(tot1[0], m0[...])))
    eliminate(gram, inverse, 0, third)
    sum2[1]()
    eliminate(gram, inverse, third, third * 2)
    sum2[2]()
    eliminate(gram, inverse, third * 2, nm // 8)
    mixing = dot(m0[...], tdot(inverse[...], rot[1]))
    picked = mine.shape[0]
    at = me * (nm // tiles)
    chosen = ones_where(
        lax.broadcasted_iota(jnp.int32, (picked, nm), 0) + at
        == lax.broadcasted_iota(jnp.int32, (picked, nm), 1)
    )
    mine[...] = lax.dot_general(
        chosen, mixing, (((1,), (1,)), ((), ())), precision=HIGH, preferred_element_type=jnp.float32
    )
    onward = pltpu.make_async_remote_copy(
        src_ref=mine, dst_ref=before, send_sem=m_send, recv_sem=m_recv,
        device_id={"cuts": nxt}, device_id_type=MESH,
    )
    onward.start()
    for row in range(rows):
        modes_out[row] = dot(f1[row, pl.ds(0, cols), :], mixing)
    sum2[3]()
    both = tot2[0]
    rayleigh_out[...] = dot(dot(mine[...], both + both.T), mixing)[: rayleigh_out.shape[0]]
    onward.wait()
    left = jnp.where(cut == 0, chosen, before[...])
    coupling_out[...] = dot(dot(left, tot2[1]), mixing)[: coupling_out.shape[0]]

    for copies in first + second:
        for cp in copies:
            cp.wait_send()
    for cp, _, _ in moved:
        cp.wait_send()
    lower.wait_send()
    upper.wait_send()


def body(start_modes, contrast, rotations, ordering):
    rows, cols, nm = start_modes.shape[1:]
    tiles = lax.axis_size("rows")
    slices = lax.axis_size("cuts")
    peers = math.isqrt(tiles)
    width = cols // 8
    cuts1 = tuple(range(0, cols + 1, width))
    count = len(cuts1) - 1
    wide = cols + 2 * PAD
    f32 = jnp.float32
    vm = lambda *shape: pltpu.VMEM(shape, f32)
    dma = lambda *shape: pltpu.SemaphoreType.DMA(shape)
    share = nm // peers
    kept = nm // tiles
    picked = max(8, kept)
    hbm = pl.BlockSpec(memory_space=pltpu.HBM)
    modes, coupling, rayleigh = pl.pallas_call(
        functools.partial(lantern_kernel, tiles=tiles, peers=peers, slices=slices, cuts1=cuts1),
        out_shape=(
            jax.ShapeDtypeStruct((rows, cols, nm), f32),
            jax.ShapeDtypeStruct((kept, nm), f32),
            jax.ShapeDtypeStruct((kept, nm), f32),
        ),
        in_specs=[hbm] * 4,
        out_specs=(pl.BlockSpec(memory_space=pltpu.VMEM),) * 3,
        scratch_shapes=[
            vm(12, wide, nm), vm(10, wide, nm), vm(8, wide, nm), vm(6, wide, nm),
            vm(12, wide, nm), vm(10, wide, nm), vm(8, wide, nm), vm(6, wide, nm),
            vm(rows, cols + PAD, nm), vm(12, cols, nm), vm(3, rows, cols), vm(nm, cols),
            vm(rows, cols, nm), vm(2, cols // 2, nm),
            vm(1, nm, nm), vm(1, nm, nm), vm(2, nm, nm),
            vm(peers, 4, share, nm), vm(peers, 4, share, nm),
            vm(1, nm, nm), vm(1, nm, nm), vm(2, nm, nm),
            vm(ITERS, nm, nm), pltpu.VMEM((ITERS, nm), jnp.int32),
            vm(nm, nm), vm(nm, nm), vm(nm, nm), vm(picked, nm), vm(picked, nm),
            dma(2), dma(2), dma(2, count), dma(2, count), dma(2, count), dma(2, count),
            dma(2), dma(2), dma(count), dma(count), dma(3, 3, peers), dma(3, 3, peers),
            pltpu.SemaphoreType.DMA, pltpu.SemaphoreType.DMA, dma(4),
        ],
        compiler_params=pltpu.CompilerParams(
            collective_id=0, has_side_effects=True, vmem_limit_bytes=40 * 1024 * 1024
        ),
        cost_estimate=pl.CostEstimate(flops=10**9, bytes_accessed=4 * 2**20, transcendentals=0),
        name="lantern",
    )(start_modes[0], contrast[0], rotations[0], ordering[0])
    return modes[None], coupling[None], rayleigh[None]


def solution(mesh):
    placed = (
        P("cuts", "rows", None, None),
        P("cuts", "rows", None),
        P("cuts", None, None, None),
        P("cuts", None, None),
    )
    return jax.shard_map(
        body,
        mesh=mesh,
        in_specs=placed,
        out_specs=(P("cuts", "rows", None, None), P("cuts", "rows", None), P("cuts", "rows", None)),
        check_vma=False,
    )
```

```python
import functools
import math

import jax
import jax.numpy as jnp
from jax import lax
from jax.experimental import pallas as pl
from jax.experimental.pallas import tpu as pltpu
from jax.sharding import PartitionSpec as P

DEGREE = 4
ITERS = 2
PAD = 8
MESH = pl.DeviceIdType.MESH
HIGH = lax.Precision.HIGHEST


def tdot(a, b):
    return lax.dot_general(
        a, b, (((0,), (0,)), ((), ())), precision=HIGH, preferred_element_type=jnp.float32
    )


def dot(a, b):
    return jnp.dot(a, b, precision=HIGH, preferred_element_type=jnp.float32)


def ones_where(condition):
    return jnp.where(condition, 1.0, 0.0).astype(jnp.float32)


def eliminate(gram, inverse, first, last):
    nm = gram.shape[0]
    row = lax.broadcasted_iota(jnp.int32, (8, nm), 0)
    for panel in range(first, last):
        o = 8 * panel
        rest = nm - o - 8
        sh, eh = gram[pl.ds(o, 8), :], inverse[pl.ds(o, 8), :]
        ch = [jnp.broadcast_to(sh[:, o + k : o + k + 1], (8, nm)) for k in range(8)]
        if rest:
            st, et = gram[pl.ds(o + 8, rest), :], inverse[pl.ds(o + 8, rest), :]
            ct = [jnp.broadcast_to(st[:, o + k : o + k + 1], (rest, nm)) for k in range(8)]
        pivots = jnp.ones((8, nm), jnp.float32)
        for j in range(8):
            pivot = ch[j][j : j + 1, :]
            scale = 1.0 / pivot
            pivots = jnp.where(row == j, pivot, pivots)
            rs, re = sh[j : j + 1, :], eh[j : j + 1, :]
            rc = [c[j : j + 1, :] for c in ch]
            mh = jnp.where(row > j, ch[j] * scale, 0.0)
            for k in range(j + 1, 8):
                ch[k] = ch[k] - mh * rc[k]
            sh = sh - mh * rs
            eh = eh - mh * re
            if rest:
                mt = ct[j] * scale
                for k in range(j + 1, 8):
                    ct[k] = ct[k] - mt * rc[k]
                st = st - mt * rs
                et = et - mt * re
        inverse[pl.ds(o, 8), :] = eh * lax.rsqrt(pivots)
        if rest:
            gram[pl.ds(o + 8, rest), :] = st
            inverse[pl.ds(o + 8, rest), :] = et


def lantern_kernel(
    v_hbm, con_hbm, rot_hbm, order_hbm, modes_out, coupling_out, rayleigh_out,
    e0, ya, yb, yc, e1, za, zb, zc, f1, coef, con, ctile, earlier, edge,
    part1, part2, landa, landb, tot1, tot2, rot, order, gram, inverse, m0, mine, before,
    con_send, con_recv, h1_send, h1_recv, h2_send, h2_recv, e_send, e_recv, x_send, x_recv,
    r_send, r_recv, m_send, m_recv, local,
    *, tiles, peers, slices, cuts1,
):
    rows, cols, nm = v_hbm.shape
    me = lax.axis_index("rows")
    cut = lax.axis_index("cuts")
    up = lax.rem(me + tiles - 1, tiles)
    down = lax.rem(me + 1, tiles)
    my = lax.rem(me, peers)
    mz = me // peers
    nxt = lax.rem(cut + 1, slices)
    prv = lax.rem(cut + slices - 1, slices)
    count = len(cuts1) - 1
    share = nm // peers

    def y_peer(d):
        return mz * peers + lax.rem(my + d, peers)

    def z_peer(d):
        return lax.rem(mz + d, peers) * peers + my

    barrier = pltpu.get_barrier_semaphore()
    for row in [up, down] + [y_peer(d) for d in range(1, peers)] + [z_peer(d) for d in range(1, peers)]:
        pl.semaphore_signal(barrier, inc=1, device_id={"rows": row}, device_id_type=MESH)
    for c in (nxt, prv):
        pl.semaphore_signal(barrier, inc=1, device_id={"cuts": c}, device_id_type=MESH)
    own_v = pltpu.make_async_copy(
        v_hbm, e0.at[pl.ds(rows, rows), pl.ds(PAD, cols), :], local.at[0]
    )
    own_v.start()
    own_c = pltpu.make_async_copy(con_hbm, con.at[1], local.at[1])
    own_c.start()
    own_r = pltpu.make_async_copy(rot_hbm, rot, local.at[2])
    own_r.start()
    own_o = pltpu.make_async_copy(order_hbm, order, local.at[3])
    own_o.start()
    pl.semaphore_wait(barrier, 2 * peers + 2)

    con_copies = []
    for side, (peer, slot) in enumerate(((up, 2), (down, 0))):
        cp = pltpu.make_async_remote_copy(
            src_ref=con_hbm, dst_ref=con.at[slot], send_sem=con_send.at[side],
            recv_sem=con_recv.at[side], device_id={"rows": peer}, device_id_type=MESH,
        )
        cp.start()
        con_copies.append(cp)

    def halo(src, dst, send, recv, index, a, b, from_hbm):
        copies = []
        for side, (peer, slot) in enumerate(((up, 2 * rows), (down, 0))):
            source = (
                src.at[:, pl.ds(a, b - a), :] if from_hbm
                else src.at[pl.ds(rows, rows), pl.ds(PAD + a, b - a), :]
            )
            cp = pltpu.make_async_remote_copy(
                src_ref=source, dst_ref=dst.at[pl.ds(slot, rows), pl.ds(PAD + a, b - a), :],
                send_sem=send.at[side, index], recv_sem=recv.at[side, index],
                device_id={"rows": peer}, device_id_type=MESH,
            )
            cp.start()
            copies.append(cp)
        return copies

    first = [
        halo(v_hbm, e0, h1_send, h1_recv, c, cuts1[c], cuts1[c + 1], True) for c in range(count)
    ]

    for ref in (e0, ya, yb, yc, e1, za, zb, zc):
        zero = jnp.zeros((ref.shape[0], PAD, nm), jnp.float32)
        ref[:, pl.ds(0, PAD), :] = zero
        ref[:, pl.ds(PAD + cols, PAD), :] = zero
    f1[:, pl.ds(cols, PAD), :] = jnp.zeros((rows, PAD, nm), jnp.float32)

    own_c.wait()
    for cp in con_copies:
        cp.wait()
    has_up = jnp.where(me > 0, 1.0, 0.0).astype(jnp.float32)
    has_down = jnp.where(me < tiles - 1, 1.0, 0.0).astype(jnp.float32)
    ctile[...] = jnp.zeros_like(ctile)
    for slot, scale in enumerate((has_up, jnp.float32(1.0), has_down)):
        ctile[pl.ds(rows * slot, rows), :] = (1.6 * con[slot] - 0.4) * scale
    for q in range(0, cols, nm):
        flipped = ctile[:, pl.ds(q, nm)].T
        for row in range(3 * rows):
            coef[row, pl.ds(q, nm), :] = jnp.broadcast_to(flipped[:, row : row + 1], (nm, nm))

    own_r.wait()
    own_o.wait()
    index = lax.broadcasted_iota(jnp.int32, (nm, nm), 0)
    for t in range(ITERS):
        picker = ones_where(index == jnp.broadcast_to(order[pl.ds(t, 1), :], (nm, nm)))
        rot[t] = dot(rot[t], picker)
    unit = ones_where(index == lax.broadcasted_iota(jnp.int32, (nm, nm), 1))

    def near(i, lo):
        return jnp.where(i < -lo, 0.4 * has_up, jnp.where(i >= rows - lo, 0.4 * has_down, 0.4))

    def stage(dst, dst_off, src, src_off, prev, prev_off, dpad, lo, hi, a, b):
        if b <= a:
            return

        def one(i, _):
            at = pl.ds(PAD + a, b - a)
            s = i + (lo + src_off)
            center = src[s, at, :]
            around = (
                src[s - 1, at, :] + src[s + 1, at, :]
                + src[s, pl.ds(PAD + a - 1, b - a), :] + src[s, pl.ds(PAD + a + 1, b - a), :]
            )
            value = coef[i + (lo + rows), pl.ds(a, b - a), :] * center + near(i, lo) * around
            if prev is None:
                value = 0.5 * value
            else:
                value = value - prev[i + (lo + prev_off), at, :]
            dst[i + (lo + dst_off), pl.ds(dpad + a, b - a), :] = value
            return 0

        lax.fori_loop(0, hi - lo, one, 0)

    def sweep_block(arrays, last, last_off, last_pad, bounds):
        e, y1, y2, y3 = arrays
        (a1, b1), (a2, b2), (a3, b3), (a4, b4) = bounds
        stage(y1, 3, e, rows, None, 0, PAD, -3, rows + 3, a1, b1)
        stage(y2, 2, y1, 3, e, rows, PAD, -2, rows + 2, a2, b2)
        stage(y3, 1, y2, 2, y1, 3, PAD, -1, rows + 1, a3, b3)
        stage(last, last_off, y3, 1, y2, 2, last_pad, 0, rows, a4, b4)

    def bounds_of(edges):
        result = []
        before = [0] * DEGREE
        for c, edge_at in enumerate(edges):
            after = [
                cols if c == len(edges) - 1 else max(0, edge_at - 8 * k) for k in range(1, DEGREE + 1)
            ]
            result.append(list(zip(before, after)))
            before = after
        return result

    def blank(ref, a, b):
        @pl.when(me == 0)
        def _():
            ref[pl.ds(0, rows), pl.ds(PAD + a, b - a), :] = jnp.zeros((rows, b - a, nm), jnp.float32)

        @pl.when(me == tiles - 1)
        def _():
            ref[pl.ds(2 * rows, rows), pl.ds(PAD + a, b - a), :] = jnp.zeros(
                (rows, b - a, nm), jnp.float32
            )

    def summing(which, part, total):
        count = part.shape[0]
        lo = (0, 0, 2)[which]
        land1 = landa.at[:, pl.ds(lo, count)]
        land2 = landb.at[:, pl.ds(lo, count)]
        ours = pl.ds(my * share, share)
        started = []

        def send(step, d, src, dst, row):
            cp = pltpu.make_async_remote_copy(
                src_ref=src, dst_ref=dst, send_sem=r_send.at[which, step, d],
                recv_sem=r_recv.at[which, step, d], device_id={"rows": row}, device_id_type=MESH,
            )
            cp.start()
            started.append(cp)

        def finish():
            for cp in started:
                cp.wait()
            started.clear()

        def added(land):
            value = land[0]
            for d in range(1, peers):
                value = value + land[d]
            return value

        def spread():
            for d in range(1, peers):
                to = pl.ds(lax.rem(my + d, peers) * share, share)
                send(0, d, part.at[:, to, :], land1.at[my], y_peer(d))
            land1[my] = part[:, ours, :]

        def across():
            finish()
            land2[mz] = added(land1)
            for d in range(1, peers):
                send(1, d, land2.at[mz], land2.at[mz], z_peer(d))

        def gather():
            finish()
            total[:, ours, :] = added(land2) * (1.0 / (rows * tiles * cols))
            for d in range(1, peers):
                send(2, d, total.at[:, ours, :], total.at[:, ours, :], y_peer(d))

        return spread, across, gather, finish

    sum1 = summing(1, part1, tot1)
    sum2 = summing(2, part2, tot2)

    own_v.wait()
    bounds1 = bounds_of(cuts1[1:])
    second = []
    for ref in (part1, part2):
        ref[...] = jnp.zeros_like(ref)
    for c in range(count):
        for cp in first[c]:
            cp.wait_recv()
        blank(e0, cuts1[c], cuts1[c + 1])
        sweep_block((e0, ya, yb, yc), e1, rows, PAD, bounds1[c])
        a, b = bounds1[c][-1]
        second.append(halo(e1, e1, h2_send, h2_recv, c, a, b, False))
        block = e1[pl.ds(rows, rows), pl.ds(PAD + a, b - a), :].reshape(rows * (b - a), nm)
        part1[1] += tdot(block, block)

    def start_inverse(value):
        gram[...] = value
        inverse[...] = unit

    def first_mixing():
        start_inverse(tot1[1])
        eliminate(gram, inverse, 0, nm // 8)
        m0[...] = tdot(inverse[...], rot[0])

    third = nm // 24

    def correlate(item):
        cp, a, b = item
        cp.wait_recv()

        @pl.when(cut == 0)
        def _():
            earlier[:, pl.ds(a, b - a), :] = e0[pl.ds(rows, rows), pl.ds(PAD + a, b - a), :]

        part2[1] += tdot(
            earlier[:, pl.ds(a, b - a), :].reshape(rows * (b - a), nm),
            f1[:, pl.ds(a, b - a), :].reshape(rows * (b - a), nm),
        )

    bounds2 = bounds_of([b[-1][1] for b in bounds1])
    moved = []
    for c in range(count):
        for cp in second[c]:
            cp.wait_recv()
        blank(e1, *bounds1[c][-1])
        sweep_block((e1, za, zb, zc), f1, 0, 0, bounds2[c])
        a, b = bounds2[c][-1]
        if b > a:
            cp = pltpu.make_async_remote_copy(
                src_ref=f1.at[:, pl.ds(a, b - a), :], dst_ref=earlier.at[:, pl.ds(a, b - a), :],
                send_sem=x_send.at[c], recv_sem=x_recv.at[c],
                device_id={"cuts": nxt}, device_id_type=MESH,
            )
            cp.start()
            moved.append((cp, a, b))
            block = f1[:, pl.ds(a, b - a), :].reshape(rows * (b - a), nm)
            part1[0] += tdot(block, block)
        if len(moved) > 2:
            correlate(moved[len(moved) - 3])
    sum1[0]()

    half = cols // 2
    lower = pltpu.make_async_remote_copy(
        src_ref=f1.at[0, pl.ds(0, half), :], dst_ref=edge.at[0],
        send_sem=e_send.at[0], recv_sem=e_recv.at[0], device_id={"rows": up}, device_id_type=MESH,
    )
    upper = pltpu.make_async_remote_copy(
        src_ref=f1.at[rows - 1, pl.ds(half, half), :], dst_ref=edge.at[1],
        send_sem=e_send.at[1], recv_sem=e_recv.at[1], device_id={"rows": down}, device_id_type=MESH,
    )
    lower.start()
    upper.start()

    for item in moved[-2:]:
        correlate(item)
    sum1[1]()
    lower.wait_recv()
    upper.wait_recv()
    for row in range(rows):
        for q in range(0, cols, half):
            at = pl.ds(q, half)
            center = f1[row, at, :]
            g = 0.25 * coef[row + rows, at, :] * center + 0.2 * f1[row, pl.ds(q + 1, half), :]
            if row < rows - 1:
                g = g + 0.2 * f1[row + 1, at, :]
            if row == rows - 1 and q == 0:
                g = g + (0.2 * has_down) * edge[0]
            if row == 0 and q > 0:
                g = g + (0.2 * has_up) * edge[1]
            part2[0] += tdot(center, g)
    sum1[2]()
    sum2[0]()

    sum1[3]()
    sum2[1]()
    first_mixing()
    start_inverse(tdot(m0[...], dot(tot1[0], m0[...])))
    eliminate(gram, inverse, 0, third)
    sum2[2]()
    eliminate(gram, inverse, third, nm // 8)
    mixing = dot(m0[...], tdot(inverse[...], rot[1]))
    picked = mine.shape[0]
    at = me * (nm // tiles)
    chosen = ones_where(
        lax.broadcasted_iota(jnp.int32, (picked, nm), 0) + at
        == lax.broadcasted_iota(jnp.int32, (picked, nm), 1)
    )
    mine[...] = lax.dot_general(
        chosen, mixing, (((1,), (1,)), ((), ())), precision=HIGH, preferred_element_type=jnp.float32
    )
    onward = pltpu.make_async_remote_copy(
        src_ref=mine, dst_ref=before, send_sem=m_send, recv_sem=m_recv,
        device_id={"cuts": nxt}, device_id_type=MESH,
    )
    onward.start()
    for row in range(rows):
        modes_out[row] = dot(f1[row, pl.ds(0, cols), :], mixing)
    sum2[3]()
    both = tot2[0]
    rayleigh_out[...] = dot(dot(mine[...], both + both.T), mixing)[: rayleigh_out.shape[0]]
    onward.wait()
    left = jnp.where(cut == 0, chosen, before[...])
    coupling_out[...] = dot(dot(left, tot2[1]), mixing)[: coupling_out.shape[0]]

    for copies in first + second:
        for cp in copies:
            cp.wait_send()
    for cp, _, _ in moved:
        cp.wait_send()
    lower.wait_send()
    upper.wait_send()


def body(start_modes, contrast, rotations, ordering):
    rows, cols, nm = start_modes.shape[1:]
    tiles = lax.axis_size("rows")
    slices = lax.axis_size("cuts")
    peers = math.isqrt(tiles)
    width = cols // 8
    cuts1 = tuple(range(0, cols + 1, width))
    count = len(cuts1) - 1
    wide = cols + 2 * PAD
    f32 = jnp.float32
    vm = lambda *shape: pltpu.VMEM(shape, f32)
    dma = lambda *shape: pltpu.SemaphoreType.DMA(shape)
    share = nm // peers
    kept = nm // tiles
    picked = max(8, kept)
    hbm = pl.BlockSpec(memory_space=pltpu.HBM)
    modes, coupling, rayleigh = pl.pallas_call(
        functools.partial(lantern_kernel, tiles=tiles, peers=peers, slices=slices, cuts1=cuts1),
        out_shape=(
            jax.ShapeDtypeStruct((rows, cols, nm), f32),
            jax.ShapeDtypeStruct((kept, nm), f32),
            jax.ShapeDtypeStruct((kept, nm), f32),
        ),
        in_specs=[hbm] * 4,
        out_specs=(pl.BlockSpec(memory_space=pltpu.VMEM),) * 3,
        scratch_shapes=[
            vm(12, wide, nm), vm(10, wide, nm), vm(8, wide, nm), vm(6, wide, nm),
            vm(12, wide, nm), vm(10, wide, nm), vm(8, wide, nm), vm(6, wide, nm),
            vm(rows, cols + PAD, nm), vm(12, cols, nm), vm(3, rows, cols), vm(nm, cols),
            vm(rows, cols, nm), vm(2, cols // 2, nm),
            vm(2, nm, nm), vm(2, nm, nm),
            vm(peers, 4, share, nm), vm(peers, 4, share, nm),
            vm(2, nm, nm), vm(2, nm, nm),
            vm(ITERS, nm, nm), pltpu.VMEM((ITERS, nm), jnp.int32),
            vm(nm, nm), vm(nm, nm), vm(nm, nm), vm(picked, nm), vm(picked, nm),
            dma(2), dma(2), dma(2, count), dma(2, count), dma(2, count), dma(2, count),
            dma(2), dma(2), dma(count), dma(count), dma(3, 3, peers), dma(3, 3, peers),
            pltpu.SemaphoreType.DMA, pltpu.SemaphoreType.DMA, dma(4),
        ],
        compiler_params=pltpu.CompilerParams(
            collective_id=0, has_side_effects=True, vmem_limit_bytes=56 * 1024 * 1024
        ),
        cost_estimate=pl.CostEstimate(flops=10**9, bytes_accessed=4 * 2**20, transcendentals=0),
        name="lantern",
    )(start_modes[0], contrast[0], rotations[0], ordering[0])
    return modes[None], coupling[None], rayleigh[None]


def solution(mesh):
    placed = (
        P("cuts", "rows", None, None),
        P("cuts", "rows", None),
        P("cuts", None, None, None),
        P("cuts", None, None),
    )
    return jax.shard_map(
        body,
        mesh=mesh,
        in_specs=placed,
        out_specs=(P("cuts", "rows", None, None), P("cuts", "rows", None), P("cuts", "rows", None)),
        check_vma=False,
    )
```

```python
import functools
import math

import jax
import jax.numpy as jnp
from jax import lax
from jax.experimental import pallas as pl
from jax.experimental.pallas import tpu as pltpu
from jax.sharding import PartitionSpec as P

DEGREE = 4
ITERS = 2
PAD = 8
MESH = pl.DeviceIdType.MESH
HIGH = lax.Precision.HIGHEST


def tdot(a, b):
    return lax.dot_general(
        a, b, (((0,), (0,)), ((), ())), precision=HIGH, preferred_element_type=jnp.float32
    )


def dot(a, b):
    return jnp.dot(a, b, precision=HIGH, preferred_element_type=jnp.float32)


def ones_where(condition):
    return jnp.where(condition, 1.0, 0.0).astype(jnp.float32)


def eliminate(gram, inverse, first, last):
    nm = gram.shape[0]
    row = lax.broadcasted_iota(jnp.int32, (8, nm), 0)
    for panel in range(first, last):
        o = 8 * panel
        rest = nm - o - 8
        sh, eh = gram[pl.ds(o, 8), :], inverse[pl.ds(o, 8), :]
        ch = [jnp.broadcast_to(sh[:, o + k : o + k + 1], (8, nm)) for k in range(8)]
        if rest:
            st, et = gram[pl.ds(o + 8, rest), :], inverse[pl.ds(o + 8, rest), :]
            ct = [jnp.broadcast_to(st[:, o + k : o + k + 1], (rest, nm)) for k in range(8)]
        pivots = jnp.ones((8, nm), jnp.float32)
        for j in range(8):
            pivot = ch[j][j : j + 1, :]
            scale = 1.0 / pivot
            pivots = jnp.where(row == j, pivot, pivots)
            rs, re = sh[j : j + 1, :], eh[j : j + 1, :]
            rc = [c[j : j + 1, :] for c in ch]
            mh = jnp.where(row > j, ch[j] * scale, 0.0)
            for k in range(j + 1, 8):
                ch[k] = ch[k] - mh * rc[k]
            sh = sh - mh * rs
            eh = eh - mh * re
            if rest:
                mt = ct[j] * scale
                for k in range(j + 1, 8):
                    ct[k] = ct[k] - mt * rc[k]
                st = st - mt * rs
                et = et - mt * re
        inverse[pl.ds(o, 8), :] = eh * lax.rsqrt(pivots)
        if rest:
            gram[pl.ds(o + 8, rest), :] = st
            inverse[pl.ds(o + 8, rest), :] = et


def lantern_kernel(
    v_hbm, con_hbm, rot_hbm, order_hbm, modes_out, coupling_out, rayleigh_out,
    e0, ya, yb, yc, e1, za, zb, zc, f1, coef, con, ctile, earlier, edge,
    part0, part1, part2, landa, landb, tot0, tot1, tot2, rot, order, gram, inverse, m0, mine, before,
    con_send, con_recv, h1_send, h1_recv, h2_send, h2_recv, e_send, e_recv, x_send, x_recv,
    r_send, r_recv, m_send, m_recv, local,
    *, tiles, peers, slices, cuts1,
):
    rows, cols, nm = v_hbm.shape
    me = lax.axis_index("rows")
    cut = lax.axis_index("cuts")
    up = lax.rem(me + tiles - 1, tiles)
    down = lax.rem(me + 1, tiles)
    my = lax.rem(me, peers)
    mz = me // peers
    nxt = lax.rem(cut + 1, slices)
    prv = lax.rem(cut + slices - 1, slices)
    count = len(cuts1) - 1
    share = nm // peers

    def y_peer(d):
        return mz * peers + lax.rem(my + d, peers)

    def z_peer(d):
        return lax.rem(mz + d, peers) * peers + my

    barrier = pltpu.get_barrier_semaphore()
    for row in [up, down] + [y_peer(d) for d in range(1, peers)] + [z_peer(d) for d in range(1, peers)]:
        pl.semaphore_signal(barrier, inc=1, device_id={"rows": row}, device_id_type=MESH)
    for c in (nxt, prv):
        pl.semaphore_signal(barrier, inc=1, device_id={"cuts": c}, device_id_type=MESH)
    own_v = pltpu.make_async_copy(
        v_hbm, e0.at[pl.ds(rows, rows), pl.ds(PAD, cols), :], local.at[0]
    )
    own_v.start()
    own_c = pltpu.make_async_copy(con_hbm, con.at[1], local.at[1])
    own_c.start()
    own_r = pltpu.make_async_copy(rot_hbm, rot, local.at[2])
    own_r.start()
    own_o = pltpu.make_async_copy(order_hbm, order, local.at[3])
    own_o.start()
    pl.semaphore_wait(barrier, 2 * peers + 2)

    con_copies = []
    for side, (peer, slot) in enumerate(((up, 2), (down, 0))):
        cp = pltpu.make_async_remote_copy(
            src_ref=con_hbm, dst_ref=con.at[slot], send_sem=con_send.at[side],
            recv_sem=con_recv.at[side], device_id={"rows": peer}, device_id_type=MESH,
        )
        cp.start()
        con_copies.append(cp)

    def halo(src, dst, send, recv, index, a, b, from_hbm):
        copies = []
        for side, (peer, slot) in enumerate(((up, 2 * rows), (down, 0))):
            source = (
                src.at[:, pl.ds(a, b - a), :] if from_hbm
                else src.at[pl.ds(rows, rows), pl.ds(PAD + a, b - a), :]
            )
            cp = pltpu.make_async_remote_copy(
                src_ref=source, dst_ref=dst.at[pl.ds(slot, rows), pl.ds(PAD + a, b - a), :],
                send_sem=send.at[side, index], recv_sem=recv.at[side, index],
                device_id={"rows": peer}, device_id_type=MESH,
            )
            cp.start()
            copies.append(cp)
        return copies

    first = [
        halo(v_hbm, e0, h1_send, h1_recv, c, cuts1[c], cuts1[c + 1], True) for c in range(count)
    ]

    for ref in (e0, ya, yb, yc, e1, za, zb, zc):
        zero = jnp.zeros((ref.shape[0], PAD, nm), jnp.float32)
        ref[:, pl.ds(0, PAD), :] = zero
        ref[:, pl.ds(PAD + cols, PAD), :] = zero
    f1[:, pl.ds(cols, PAD), :] = jnp.zeros((rows, PAD, nm), jnp.float32)

    own_c.wait()
    for cp in con_copies:
        cp.wait()
    has_up = jnp.where(me > 0, 1.0, 0.0).astype(jnp.float32)
    has_down = jnp.where(me < tiles - 1, 1.0, 0.0).astype(jnp.float32)
    ctile[...] = jnp.zeros_like(ctile)
    for slot, scale in enumerate((has_up, jnp.float32(1.0), has_down)):
        ctile[pl.ds(rows * slot, rows), :] = (1.6 * con[slot] - 0.4) * scale
    for q in range(0, cols, nm):
        flipped = ctile[:, pl.ds(q, nm)].T
        for row in range(3 * rows):
            coef[row, pl.ds(q, nm), :] = jnp.broadcast_to(flipped[:, row : row + 1], (nm, nm))

    own_r.wait()
    own_o.wait()
    index = lax.broadcasted_iota(jnp.int32, (nm, nm), 0)
    for t in range(ITERS):
        picker = ones_where(index == jnp.broadcast_to(order[pl.ds(t, 1), :], (nm, nm)))
        rot[t] = dot(rot[t], picker)
    unit = ones_where(index == lax.broadcasted_iota(jnp.int32, (nm, nm), 1))

    def near(i, lo):
        return jnp.where(i < -lo, 0.4 * has_up, jnp.where(i >= rows - lo, 0.4 * has_down, 0.4))

    def stage(dst, dst_off, src, src_off, prev, prev_off, dpad, lo, hi, a, b):
        if b <= a:
            return

        def one(i, _):
            at = pl.ds(PAD + a, b - a)
            s = i + (lo + src_off)
            center = src[s, at, :]
            around = (
                src[s - 1, at, :] + src[s + 1, at, :]
                + src[s, pl.ds(PAD + a - 1, b - a), :] + src[s, pl.ds(PAD + a + 1, b - a), :]
            )
            value = coef[i + (lo + rows), pl.ds(a, b - a), :] * center + near(i, lo) * around
            if prev is None:
                value = 0.5 * value
            else:
                value = value - prev[i + (lo + prev_off), at, :]
            dst[i + (lo + dst_off), pl.ds(dpad + a, b - a), :] = value
            return 0

        lax.fori_loop(0, hi - lo, one, 0)

    def sweep_block(arrays, last, last_off, last_pad, bounds):
        e, y1, y2, y3 = arrays
        (a1, b1), (a2, b2), (a3, b3), (a4, b4) = bounds
        stage(y1, 3, e, rows, None, 0, PAD, -3, rows + 3, a1, b1)
        stage(y2, 2, y1, 3, e, rows, PAD, -2, rows + 2, a2, b2)
        stage(y3, 1, y2, 2, y1, 3, PAD, -1, rows + 1, a3, b3)
        stage(last, last_off, y3, 1, y2, 2, last_pad, 0, rows, a4, b4)

    def bounds_of(edges):
        result = []
        before = [0] * DEGREE
        for c, edge_at in enumerate(edges):
            after = [
                cols if c == len(edges) - 1 else max(0, edge_at - 8 * k) for k in range(1, DEGREE + 1)
            ]
            result.append(list(zip(before, after)))
            before = after
        return result

    def blank(ref, a, b):
        @pl.when(me == 0)
        def _():
            ref[pl.ds(0, rows), pl.ds(PAD + a, b - a), :] = jnp.zeros((rows, b - a, nm), jnp.float32)

        @pl.when(me == tiles - 1)
        def _():
            ref[pl.ds(2 * rows, rows), pl.ds(PAD + a, b - a), :] = jnp.zeros(
                (rows, b - a, nm), jnp.float32
            )

    def summing(which, part, total):
        count = part.shape[0]
        lo = (0, 1, 2)[which]
        land1 = landa.at[:, pl.ds(lo, count)]
        land2 = landb.at[:, pl.ds(lo, count)]
        ours = pl.ds(my * share, share)
        started = []

        def send(step, d, src, dst, row):
            cp = pltpu.make_async_remote_copy(
                src_ref=src, dst_ref=dst, send_sem=r_send.at[which, step, d],
                recv_sem=r_recv.at[which, step, d], device_id={"rows": row}, device_id_type=MESH,
            )
            cp.start()
            started.append(cp)

        def finish():
            for cp in started:
                cp.wait()
            started.clear()

        def added(land):
            value = land[0]
            for d in range(1, peers):
                value = value + land[d]
            return value

        def spread():
            for d in range(1, peers):
                to = pl.ds(lax.rem(my + d, peers) * share, share)
                send(0, d, part.at[:, to, :], land1.at[my], y_peer(d))
            land1[my] = part[:, ours, :]

        def across():
            finish()
            land2[mz] = added(land1)
            for d in range(1, peers):
                send(1, d, land2.at[mz], land2.at[mz], z_peer(d))

        def gather():
            finish()
            total[:, ours, :] = added(land2) * (1.0 / (rows * tiles * cols))
            for d in range(1, peers):
                send(2, d, total.at[:, ours, :], total.at[:, ours, :], y_peer(d))

        return spread, across, gather, finish

    sum0 = summing(0, part0, tot0)
    sum1 = summing(1, part1, tot1)
    sum2 = summing(2, part2, tot2)

    own_v.wait()
    bounds1 = bounds_of(cuts1[1:])
    second = []
    for ref in (part0, part1, part2):
        ref[...] = jnp.zeros_like(ref)
    for c in range(count):
        for cp in first[c]:
            cp.wait_recv()
        blank(e0, cuts1[c], cuts1[c + 1])
        sweep_block((e0, ya, yb, yc), e1, rows, PAD, bounds1[c])
        a, b = bounds1[c][-1]
        second.append(halo(e1, e1, h2_send, h2_recv, c, a, b, False))
        block = e1[pl.ds(rows, rows), pl.ds(PAD + a, b - a), :].reshape(rows * (b - a), nm)
        part0[0] += tdot(block, block)
    sum0[0]()

    def start_inverse(value):
        gram[...] = value
        inverse[...] = unit

    def first_mixing():
        start_inverse(tot0[0])
        eliminate(gram, inverse, 0, nm // 8)
        m0[...] = tdot(inverse[...], rot[0])

    third = nm // 24

    def correlate(item):
        cp, a, b = item
        cp.wait_recv()

        @pl.when(cut == 0)
        def _():
            earlier[:, pl.ds(a, b - a), :] = e0[pl.ds(rows, rows), pl.ds(PAD + a, b - a), :]

        part2[1] += tdot(
            earlier[:, pl.ds(a, b - a), :].reshape(rows * (b - a), nm),
            f1[:, pl.ds(a, b - a), :].reshape(rows * (b - a), nm),
        )

    bounds2 = bounds_of([b[-1][1] for b in bounds1])
    moved = []
    for c in range(count):
        for cp in second[c]:
            cp.wait_recv()
        blank(e1, *bounds1[c][-1])
        sweep_block((e1, za, zb, zc), f1, 0, 0, bounds2[c])
        a, b = bounds2[c][-1]
        if b > a:
            cp = pltpu.make_async_remote_copy(
                src_ref=f1.at[:, pl.ds(a, b - a), :], dst_ref=earlier.at[:, pl.ds(a, b - a), :],
                send_sem=x_send.at[c], recv_sem=x_recv.at[c],
                device_id={"cuts": nxt}, device_id_type=MESH,
            )
            cp.start()
            moved.append((cp, a, b))
            block = f1[:, pl.ds(a, b - a), :].reshape(rows * (b - a), nm)
            part1[0] += tdot(block, block)
        if len(moved) > 2:
            correlate(moved[len(moved) - 3])
    sum1[0]()

    half = cols // 2
    lower = pltpu.make_async_remote_copy(
        src_ref=f1.at[0, pl.ds(0, half), :], dst_ref=edge.at[0],
        send_sem=e_send.at[0], recv_sem=e_recv.at[0], device_id={"rows": up}, device_id_type=MESH,
    )
    upper = pltpu.make_async_remote_copy(
        src_ref=f1.at[rows - 1, pl.ds(half, half), :], dst_ref=edge.at[1],
        send_sem=e_send.at[1], recv_sem=e_recv.at[1], device_id={"rows": down}, device_id_type=MESH,
    )
    lower.start()
    upper.start()
    sum0[1]()

    for item in moved[-2:]:
        correlate(item)
    sum1[1]()
    sum0[2]()
    lower.wait_recv()
    upper.wait_recv()
    for row in range(rows):
        for q in range(0, cols, half):
            at = pl.ds(q, half)
            center = f1[row, at, :]
            g = 0.25 * coef[row + rows, at, :] * center + 0.2 * f1[row, pl.ds(q + 1, half), :]
            if row < rows - 1:
                g = g + 0.2 * f1[row + 1, at, :]
            if row == rows - 1 and q == 0:
                g = g + (0.2 * has_down) * edge[0]
            if row == 0 and q > 0:
                g = g + (0.2 * has_up) * edge[1]
            part2[0] += tdot(center, g)
    sum2[0]()
    sum1[2]()
    sum0[3]()
    first_mixing()
    sum2[1]()

    sum1[3]()
    start_inverse(tdot(m0[...], dot(tot1[0], m0[...])))
    eliminate(gram, inverse, 0, third)
    sum2[2]()
    eliminate(gram, inverse, third, nm // 8)
    mixing = dot(m0[...], tdot(inverse[...], rot[1]))
    picked = mine.shape[0]
    at = me * (nm // tiles)
    chosen = ones_where(
        lax.broadcasted_iota(jnp.int32, (picked, nm), 0) + at
        == lax.broadcasted_iota(jnp.int32, (picked, nm), 1)
    )
    mine[...] = lax.dot_general(
        chosen, mixing, (((1,), (1,)), ((), ())), precision=HIGH, preferred_element_type=jnp.float32
    )
    onward = pltpu.make_async_remote_copy(
        src_ref=mine, dst_ref=before, send_sem=m_send, recv_sem=m_recv,
        device_id={"cuts": nxt}, device_id_type=MESH,
    )
    onward.start()
    for row in range(rows):
        modes_out[row] = dot(f1[row, pl.ds(0, cols), :], mixing)
    sum2[3]()
    both = tot2[0]
    rayleigh_out[...] = dot(dot(mine[...], both + both.T), mixing)[: rayleigh_out.shape[0]]
    onward.wait()
    left = jnp.where(cut == 0, chosen, before[...])
    coupling_out[...] = dot(dot(left, tot2[1]), mixing)[: coupling_out.shape[0]]

    for copies in first + second:
        for cp in copies:
            cp.wait_send()
    for cp, _, _ in moved:
        cp.wait_send()
    lower.wait_send()
    upper.wait_send()


def body(start_modes, contrast, rotations, ordering):
    rows, cols, nm = start_modes.shape[1:]
    tiles = lax.axis_size("rows")
    slices = lax.axis_size("cuts")
    peers = math.isqrt(tiles)
    width = cols // 8
    cuts1 = tuple(range(0, cols + 1, width))
    count = len(cuts1) - 1
    wide = cols + 2 * PAD
    f32 = jnp.float32
    vm = lambda *shape: pltpu.VMEM(shape, f32)
    dma = lambda *shape: pltpu.SemaphoreType.DMA(shape)
    share = nm // peers
    kept = nm // tiles
    picked = max(8, kept)
    hbm = pl.BlockSpec(memory_space=pltpu.HBM)
    modes, coupling, rayleigh = pl.pallas_call(
        functools.partial(lantern_kernel, tiles=tiles, peers=peers, slices=slices, cuts1=cuts1),
        out_shape=(
            jax.ShapeDtypeStruct((rows, cols, nm), f32),
            jax.ShapeDtypeStruct((kept, nm), f32),
            jax.ShapeDtypeStruct((kept, nm), f32),
        ),
        in_specs=[hbm] * 4,
        out_specs=(pl.BlockSpec(memory_space=pltpu.VMEM),) * 3,
        scratch_shapes=[
            vm(12, wide, nm), vm(10, wide, nm), vm(8, wide, nm), vm(6, wide, nm),
            vm(12, wide, nm), vm(10, wide, nm), vm(8, wide, nm), vm(6, wide, nm),
            vm(rows, cols + PAD, nm), vm(12, cols, nm), vm(3, rows, cols), vm(nm, cols),
            vm(rows, cols, nm), vm(2, cols // 2, nm),
            vm(1, nm, nm), vm(1, nm, nm), vm(2, nm, nm),
            vm(peers, 4, share, nm), vm(peers, 4, share, nm),
            vm(1, nm, nm), vm(1, nm, nm), vm(2, nm, nm),
            vm(ITERS, nm, nm), pltpu.VMEM((ITERS, nm), jnp.int32),
            vm(nm, nm), vm(nm, nm), vm(nm, nm), vm(picked, nm), vm(picked, nm),
            dma(2), dma(2), dma(2, count), dma(2, count), dma(2, count), dma(2, count),
            dma(2), dma(2), dma(count), dma(count), dma(3, 3, peers), dma(3, 3, peers),
            pltpu.SemaphoreType.DMA, pltpu.SemaphoreType.DMA, dma(4),
        ],
        compiler_params=pltpu.CompilerParams(
            collective_id=0, has_side_effects=True, vmem_limit_bytes=56 * 1024 * 1024
        ),
        cost_estimate=pl.CostEstimate(flops=10**9, bytes_accessed=4 * 2**20, transcendentals=0),
        name="lantern",
    )(start_modes[0], contrast[0], rotations[0], ordering[0])
    return modes[None], coupling[None], rayleigh[None]


def solution(mesh):
    placed = (
        P("cuts", "rows", None, None),
        P("cuts", "rows", None),
        P("cuts", None, None, None),
        P("cuts", None, None),
    )
    return jax.shard_map(
        body,
        mesh=mesh,
        in_specs=placed,
        out_specs=(P("cuts", "rows", None, None), P("cuts", "rows", None), P("cuts", "rows", None)),
        check_vma=False,
    )
```
